512 devices in a mesh: rep: 16 (over z), head: 32 (over x, y, core).
Axes of the slice: x: 4, y: 4, z: 16, core: 2. Of those that a mesh axis runs over, the one named last changes fastest.
Arguments:
- layer_input: bfloat16 [8192, 8192], P('rep', 'head'), may hold values from -6 to 6
- proj_weight: bfloat16 [8192, 8192], P('rep', 'head'), may hold values from -0.0625 to 0.0625
- step_weight: bfloat16 [8192, 128], P('rep', 'head'), may hold values from -0.0625 to 0.0625
- step_bias: float32 [128], P('head'), may hold values from -4 to 0.5
- decay_log: float32 [128], P('head'), may hold values from -7 to -1
- conv_weight: float32 [4, 8192], P(None, 'head'), may hold values from -3 to 3
- conv_bias: float32 [8192], P('head'), may hold values from -2 to 2
- skip_gain: float32 [128], P('head'), may hold values from 0.5 to 1.5
- group_inputs: bfloat16 [8192, 2048], P('rep', 'head'), may hold values from -1.5 to 1.5
- cached_state: float32 [16, 128, 64, 256], P('rep', 'head'), may hold values from -1.5 to 1.5
- cached_tail: float32 [16, 3, 8192], P('rep', None, 'head'), may hold values from -6 to 6
- owner_map: int32 [16], replicated, may hold values from 0 to 15, each once
- request_state: int32 [16], replicated, may hold values from 0 to 16, as said below
- shared_id: int32 [1], replicated, may hold values from 0 to 15
Outputs:
- ssm_output: bfloat16 [8192, 8192], P('rep', 'head')
- final_state: float32 [16, 128, 64, 256], P('rep', 'head')
- final_tail: float32 [16, 3, 8192], P('rep', None, 'head')
The draws below stay inside these ranges and needn't reach their ends.
Inputs may be any that keep to these rules, and one draw needn't show every extreme that they name: `request_state`: A value below 16 is a state id; the value 16 means the shared prompt, whose id is shared_id; some request always names it. `owner_map`: each state id has its own cache row.
All inputs are finite; a program needn't handle non-finite values.
Results may differ from the reference program's by a relative error of at most 0.015.
Values may be sent and summed in bfloat16 or wider, within the bound.
A program may use at most 128 MiB of HBM per device.

```python
import jax
import jax.numpy as jnp
from jax import lax

D = 8192
HEADS = 128
P_SIZE = 64
N = 256
G = 4
KERNEL = 4
NEW_TOK = 512
REQUESTS = 16
IDS = 16
TOKENS = 8192
CHAN = 8192


def draw_request_state(key, part):
    key = jax.random.fold_in(key, 7)
    first_key, second_key = jax.random.split(key, 2)
    chosen = jax.random.randint(first_key, (REQUESTS,), 0, IDS + 1)
    forced = jax.random.randint(second_key, (), 0, REQUESTS)
    chosen = chosen.at[forced].set(IDS)
    return chosen.astype(jnp.int32)


def steps_of(own_key, shape, cuts, smallest, high):
    def one(axis_at, parts):
        steps = jax.random.uniform(jax.random.fold_in(jax.random.fold_in(own_key, 6), axis_at), (parts,), jnp.float32, smallest / len(cuts), high / len(cuts))
        return jnp.repeat(jnp.exp(steps), shape[axis_at] // parts).reshape((-1,) + (1,) * (len(shape) - axis_at - 1))

    level = one(*cuts[0])
    for cut in cuts[1:]:
        level = level * one(*cut)
    return level


def bell_draw(rng, extent, width, most, cuts=(), kind=jnp.bfloat16):
    values = jax.random.normal(rng, extent, jnp.float32) * width
    if len(cuts) > 0:
        values = steps_of(rng, extent, cuts, -0.22, 0.18) * values
    return jnp.clip(values, min=-most, max=most).astype(kind)


def setup_inputs(seed: int = 0) -> dict:
    keys = jax.random.split(jax.random.key(seed), 15)
    return {
        "layer_input": bell_draw(keys[0], (TOKENS, D), 1.0, 6.0, ((0, 16), (1, 32))),
        "proj_weight": bell_draw(keys[1], (D, CHAN), D ** -0.5, 0.0625, ((0, 16), (1, 32))),
        "step_weight": bell_draw(keys[2], (D, HEADS), D ** -0.5, 0.0625, ((0, 16), (1, 32))),
        "step_bias": jnp.clip(-4.0 + 4.5 * jax.random.uniform(keys[3], (HEADS,), jnp.float32) ** steps_of(keys[3], (HEADS,), ((0, 32),), -0.2, 0.2), -4.0, 0.5),
        "decay_log": jnp.clip(-7.0 + 6.0 * jax.random.uniform(keys[4], (HEADS,), jnp.float32) ** steps_of(keys[4], (HEADS,), ((0, 32),), -0.2, 0.2), -7.0, -1.0),
        "conv_weight": bell_draw(keys[5], (KERNEL, CHAN), 0.5, 3.0, ((1, 32),), jnp.float32),
        "conv_bias": bell_draw(keys[6], (CHAN,), 0.3, 2.0, ((0, 32),), jnp.float32),
        "skip_gain": jnp.clip(0.5 + 1.0 * jax.random.uniform(keys[7], (HEADS,), jnp.float32) ** steps_of(keys[7], (HEADS,), ((0, 32),), -0.2, 0.2), 0.5, 1.5),
        "group_inputs": bell_draw(keys[8], (TOKENS, 2 * G * N), 0.25, 1.5, ((0, 16), (1, 32))),
        "cached_state": bell_draw(keys[9], (IDS, HEADS, P_SIZE, N), 0.25, 1.5, ((0, 16), (1, 32)), jnp.float32),
        "cached_tail": bell_draw(keys[10], (IDS, KERNEL - 1, CHAN), 1.0, 6.0, ((0, 16), (2, 32)), jnp.float32),
        "owner_map": jax.random.permutation(keys[11], IDS).astype(jnp.int32),
        "request_state": draw_request_state(jax.random.fold_in(keys[14], 71), 0),
        "shared_id": jax.random.randint(keys[13], (1,), 0, IDS).astype(jnp.int32),
    }


def one_request(operands, step_bias, decay_log, conv_weight, conv_bias, skip_gain):
    projected, step_raw, group_rows, prior_state, prior_tail = operands
    step_size = jax.nn.softplus(step_raw + step_bias)
    extended = jnp.concatenate([prior_tail, projected.astype(jnp.float32)], axis=0)
    final_tail = extended[NEW_TOK:]
    conv_sum = conv_bias + conv_weight[0] * extended[0:NEW_TOK]
    for offset in range(1, KERNEL):
        conv_sum = conv_sum + conv_weight[offset] * extended[offset:offset + NEW_TOK]
    conv_out = jax.nn.silu(conv_sum).astype(jnp.bfloat16)
    decay_sum = jnp.cumsum(-jnp.exp(decay_log) * step_size, axis=0)
    grouped = group_rows.reshape(NEW_TOK, G, 2, N)
    per_group = HEADS // G
    in_vec = jnp.repeat(grouped[:, :, 0, :], per_group, axis=1)
    out_vec = jnp.repeat(grouped[:, :, 1, :], per_group, axis=1)
    scores = jnp.einsum('thn,shn->hts', out_vec.astype(jnp.float32), in_vec.astype(jnp.float32))
    lower = jnp.tril(jnp.ones((NEW_TOK, NEW_TOK), dtype=bool))
    differ = decay_sum.T[:, :, None] - decay_sum.T[:, None, :]
    decays = jnp.where(lower[None], jnp.exp(jnp.where(lower[None], differ, 0.0)), 0.0)
    mixing = (scores * decays * step_size.T[:, None, :]).astype(jnp.bfloat16)
    heads_x = conv_out.reshape(NEW_TOK, HEADS, P_SIZE)
    inner = jnp.einsum('hts,shp->thp', mixing.astype(jnp.float32), heads_x.astype(jnp.float32))
    carried = jnp.einsum('thn,hpn->thp', out_vec.astype(jnp.float32), prior_state, precision=lax.Precision.HIGHEST)
    carried = carried * jnp.exp(decay_sum)[:, :, None]
    output = inner + carried + skip_gain[None, :, None] * heads_x.astype(jnp.float32)
    output = output.reshape(NEW_TOK, HEADS * P_SIZE).astype(jnp.bfloat16)
    last = decay_sum[NEW_TOK - 1]
    weights = jnp.exp(last[None, :] - decay_sum) * step_size
    weighted = (heads_x.astype(jnp.float32) * weights[:, :, None]).astype(jnp.bfloat16)
    final_state = jnp.exp(last)[:, None, None] * prior_state + jnp.einsum('thp,thn->hpn', weighted.astype(jnp.float32), in_vec.astype(jnp.float32))
    return output, final_state, final_tail


def reference(layer_input, proj_weight, step_weight, step_bias, decay_log, conv_weight, conv_bias, skip_gain, group_inputs, cached_state, cached_tail, owner_map, request_state, shared_id):
    projected = jnp.dot(layer_input, proj_weight, preferred_element_type=jnp.float32).astype(jnp.bfloat16)
    step_raw = jnp.dot(layer_input, step_weight, preferred_element_type=jnp.float32)
    state_ids = jnp.where(request_state < IDS, request_state, shared_id[0]).astype(jnp.int32)
    state_row = owner_map[state_ids].astype(jnp.int32)
    prior_state = cached_state[state_row]
    prior_tail = cached_tail[state_row]
    stacked = (projected.reshape(REQUESTS, NEW_TOK, HEADS * P_SIZE), step_raw.reshape(REQUESTS, NEW_TOK, HEADS), group_inputs.reshape(REQUESTS, NEW_TOK, 2 * G * N), prior_state, prior_tail)
    output, final_state, final_tail = lax.map(lambda operands: one_request(operands, step_bias, decay_log, conv_weight, conv_bias, skip_gain), stacked)
    return output.reshape(TOKENS, HEADS * P_SIZE), final_state, final_tail
```

```python
import jax
import jax.numpy as jnp
from jax import lax
from jax.experimental import pallas as pl
from jax.experimental.pallas import tpu as pltpu
from jax.sharding import PartitionSpec as P

MESH = pl.DeviceIdType.MESH
BF = jnp.bfloat16
F32 = jnp.float32
Z = 16
TOK = 512
CH = 256
HEADS = 4
N = 256
WSUB = 4
SSUB = 2


def body(
    request_state, owner_map, shared_id, step_bias, decay_log, skip_gain,
    x_hbm, w_hbm, misc_in, state_hbm, g_hbm, conv_w, conv_b,
    out_ref, fstate_ref, ftail_ref,
    A, W, S, M, G, state_own, g_own, acc, sacc, ext, inT, outv, score, mix, xbd,
    loc_sem, ws_sem, wr_sem, ss_sem, sr_sem, ms_sem, mr_sem, as_sem, ar_sem, cs_sem, cr_sem, gs_sem, gr_sem,
):
    z = lax.axis_index("rep")
    hid = lax.axis_index("head")
    x, y, c = hid // 8, (hid // 2) % 4, hid % 2
    zr, zl = (z + 1) % Z, (z + Z - 1) % Z

    def dev(xx, yy, cc):
        return {"head": xx * 8 + yy * 2 + cc}

    xp, xm, yp, ym = (x + 1) % 4, (x + 3) % 4, (y + 1) % 4, (y + 3) % 4
    sibling = dev(x, y, 1 - c)
    zdev = ({"rep": zr}, {"rep": zl})
    pos = ((y, x), (x, y))
    x_nb, y_nb = (dev(xp, y, c), dev(xm, y, c)), (dev(x, yp, c), dev(x, ym, c))
    q_nb, p_nb = (x_nb, y_nb), (y_nb, x_nb)

    locs = [
        pltpu.make_async_copy(g_hbm, g_own, loc_sem.at[0]),
        pltpu.make_async_copy(x_hbm.at[0:256], A.at[0, c, y, x], loc_sem.at[1]),
        pltpu.make_async_copy(x_hbm.at[256:512], A.at[1, c, x, y], loc_sem.at[2]),
        pltpu.make_async_copy(w_hbm, W.at[0], loc_sem.at[3]),
        pltpu.make_async_copy(state_hbm, state_own, loc_sem.at[4]),
        pltpu.make_async_copy(misc_in, M.at[0], loc_sem.at[5]),
    ]
    for copy in locs:
        copy.start()

    barrier = pltpu.get_barrier_semaphore()
    for d in (*zdev, *x_nb, *y_nb, sibling):
        pl.semaphore_signal(barrier, inc=1, device_id=d, device_id_type=MESH)

    locs[0].wait()
    g_wide = jnp.concatenate([g_own[...].astype(F32), jnp.zeros((TOK, 64), F32)], axis=1)
    G[c, y] = g_wide.T[0:64].astype(BF)
    locs[4].wait()
    S[0] = state_own[...].astype(BF)
    for i in (1, 2, 3, 5):
        locs[i].wait()
    pl.semaphore_wait(barrier, 7)

    sends = []

    def rcopy(src, dst, s_sem, r_sem, d):
        return pltpu.make_async_remote_copy(
            src_ref=src, dst_ref=dst, send_sem=s_sem, recv_sem=r_sem, device_id=d, device_id_type=MESH
        )

    def go(ref, s_sem, r_sem, d, dst=None):
        copy = rcopy(ref, ref if dst is None else dst, s_sem, r_sem, d)
        copy.start()
        sends.append(copy)

    def got(ref, s_sem, r_sem, d):
        rcopy(ref, ref, s_sem, r_sem, d).wait_recv()

    def slot(way, s):
        return s if way == 0 else (Z - s) % Z

    def ring(buf, rows, sub, s_sem, r_sem, way, s):
        here = buf.at[slot(way, s), rows]
        if s > 0:
            got(here, s_sem.at[way, s - 1, sub], r_sem.at[way, s - 1, sub], zdev[way])
        if s < 8 and not (s == 7 and sub not in last_subs(way, s_sem)):
            go(here, s_sem.at[way, s, sub], r_sem.at[way, s, sub], zdev[way], buf.at[slot(way, s + 1), rows])

    def last_subs(way, s_sem):
        if s_sem is ws_sem:
            return (0, 1) if way == 0 else (2, 3)
        if s_sem is ss_sem:
            return (0,) if way == 0 else (1,)
        return (0,) if way == 0 else ()

    def w_step(s, subs=range(WSUB)):
        for sub in subs:
            for way in (0, 1):
                if s < 8 or sub in last_subs(way, ws_sem):
                    ring(W, pl.ds(sub * (512 // WSUB), 512 // WSUB), sub, ws_sem, wr_sem, way, s)

    def s_step(s, subs=range(SSUB)):
        for sub in subs:
            for way in (0, 1):
                if s < 8 or sub in last_subs(way, ss_sem):
                    ring(S, pl.ds(sub * (256 // SSUB), 256 // SSUB), sub, ss_sem, sr_sem, way, s)

    def m_step(s):
        for way in (0, 1):
            if s < 8 or 0 in last_subs(way, ms_sem):
                ring(M, pl.ds(0, 16), 0, ms_sem, mr_sem, way, s)

    def ring4(stage, blk, halves, nb, s_sem, r_sem):
        if stage == 0:
            for way in (0, 1):
                go(blk(0), s_sem.at[way], r_sem.at[way], nb[way])
        elif stage == 1:
            for way, step in ((0, -1), (1, 1)):
                got(blk(step), s_sem.at[way], r_sem.at[way], nb[way])
                go(halves(blk(step), way), s_sem.at[2 + way], r_sem.at[2 + way], nb[way])
        else:
            for way in (0, 1):
                got(halves(blk(2), way), s_sem.at[2 + way], r_sem.at[2 + way], nb[way])

    def a_one(stage, i):
        p, q = pos[i]
        ring4(
            stage,
            lambda k: A.at[i, c, p, (q + 4 + k) % 4],
            lambda ref, way: ref.at[pl.ds(128 * way, 128)],
            q_nb[i], as_sem.at[i, 0], ar_sem.at[i, 0],
        )

    def a_two(stage, i):
        p, _ = pos[i]
        ring4(
            stage,
            lambda k: A.at[i, c, (p + 4 + k) % 4],
            lambda ref, way: ref.at[pl.ds(2 * way, 2)],
            p_nb[i], as_sem.at[i, 1], ar_sem.at[i, 1],
        )

    def a_share(i, k):
        p, _ = pos[i]
        go(A.at[i, c, (p + k) % 4], cs_sem.at[i, k], cr_sem.at[i, k], sibling)

    def a_shared(i, k):
        p, _ = pos[i]
        got(A.at[i, 1 - c, (p + k) % 4], cs_sem.at[i, k], cr_sem.at[i, k], sibling)

    def g_ring(stage):
        ring4(
            stage,
            lambda k: G.at[c, (y + 4 + k) % 4],
            lambda ref, way: ref.at[pl.ds(32 * way, 32)],
            y_nb, gs_sem, gr_sem,
        )

    def a_block(i, kz, cc):
        ax, ay = kz // 4, kz % 4
        return A[0, cc, ay, ax] if i == 0 else A[1, cc, ax, ay]

    def project(j):
        kz = (z - j + Z) % Z
        for i in (0, 1):
            rows = pl.ds(256 * i, 256)
            part = jnp.dot(a_block(i, kz, 0), W[j, 0:256], preferred_element_type=F32)
            part += jnp.dot(a_block(i, kz, 1), W[j, 256:512], preferred_element_type=F32)
            acc[rows, :] += part

    def step_part(j):
        kz = (z - j + Z) % Z
        for i in (0, 1):
            for cc in (0, 1):
                sacc[cc, :, pl.ds(256 * i, 256)] += lax.dot_general(
                    M[j], a_block(i, kz, cc), (((1,), (1,)), ((), ())), preferred_element_type=F32
                )

    m_step(0)
    for i in (0, 1):
        a_one(0, i)
    g_ring(0)
    s_step(0)
    w_step(0)
    acc[...] = jnp.zeros_like(acc)
    sacc[...] = jnp.zeros_like(sacc)
    m_step(1)
    for i in (0, 1):
        a_one(1, i)
    g_ring(1)
    for i in (0, 1):
        a_one(2, i)
        a_two(0, i)
        a_share(i, 0)
    g_ring(2)
    go(G.at[c], gs_sem.at[4], gr_sem.at[4], sibling)
    m_step(2)
    s_step(1)
    w_step(1)
    m_step(3)
    got(G.at[1 - c], gs_sem.at[4], gr_sem.at[4], sibling)
    for k in range(4):
        inT[pl.ds(64 * k, 64), :] = G[k % 2, k // 2]
        outv[:, pl.ds(64 * k, 64)] = G[k % 2, 2 + k // 2].astype(F32).T.astype(BF)
    for tb in range(4):
        t0 = tb * 128
        cols = 256 if tb < 2 else 512
        sc = jnp.dot(outv[pl.ds(t0, 128), :], inT[:, 0:cols], preferred_element_type=F32)
        keep = lax.broadcasted_iota(jnp.int32, (128, cols), 1) <= t0 + lax.broadcasted_iota(jnp.int32, (128, cols), 0)
        score[pl.ds(t0, 128), 0:cols] = jnp.where(keep, sc, 0.0)
    m_step(4)
    for i in (0, 1):
        a_two(1, i)
        a_share(i, 3)
        a_share(i, 1)
    s_step(2)
    w_step(2)
    m_step(5)
    for i in (0, 1):
        a_two(2, i)
        a_share(i, 2)
    s_step(3)
    w_step(3)
    m_step(6)
    m_step(7)
    for i in (0, 1):
        for k in range(4):
            a_shared(i, k)
    s_step(4)
    w_step(4)
    m_step(8)

    @pl.loop(0, Z)
    def _(j):
        step_part(j)

    project(0)

    @pl.loop(1, 5)
    def _(j):
        project(j)
        project(Z - j)

    row = lax.broadcasted_iota(jnp.int32, (8, 1), 0)

    def per_head(ref):
        col = jnp.zeros((8, 1), F32)
        for h in range(HEADS):
            col = jnp.where(row == h, ref[h], col)
        return col

    raw = jnp.concatenate([sacc[0, 0:4] + sacc[1, 4:8], jnp.zeros((4, TOK), F32)], axis=0)
    raw = raw + per_head(step_bias)
    step = jnp.maximum(raw, 0.0) + jnp.log1p(jnp.exp(-jnp.abs(raw)))
    decay = -jnp.exp(per_head(decay_log)) * step
    lane = lax.broadcasted_iota(jnp.int32, (8, TOK), 1)
    for k in range(9):
        decay = decay + jnp.where(lane >= 2**k, pltpu.roll(decay, 2**k, axis=1), 0.0)
    last = decay[:, TOK - 1 : TOK]
    weights = jnp.exp(last - decay) * step
    decay_t = jnp.concatenate([decay, jnp.zeros((120, TOK), F32)], axis=0).T
    grown_t = jnp.exp(decay_t)
    weights_t = jnp.concatenate([weights, jnp.zeros((120, TOK), F32)], axis=0).T
    s_step(5)
    w_step(5)
    project(5)
    project(Z - 5)

    def make_mix(h):
        for tb in range(4):
            t0 = tb * 128
            cols = 256 if tb < 2 else 512
            differ = decay_t[t0 : t0 + 128, h : h + 1] - decay[h : h + 1, 0:cols]
            scaled = jnp.exp(jnp.minimum(differ, 0.0)) * step[h : h + 1, 0:cols]
            mix[h, pl.ds(t0, 128), 0:cols] = (score[pl.ds(t0, 128), 0:cols] * scaled).astype(BF)

    make_mix(0)
    make_mix(1)
    s_step(6)
    w_step(6)
    project(6)
    project(Z - 6)
    make_mix(2)
    make_mix(3)
    s_step(7)
    w_step(7)
    project(7)
    project(Z - 7)

    chan = lax.broadcasted_iota(jnp.int32, (TOK, CH), 1) // 64

    def expand(cols):
        wide = jnp.broadcast_to(cols[:, 0:1], (TOK, CH))
        for h in range(1, HEADS):
            wide = jnp.where(chan == h, cols[:, h : h + 1], wide)
        return wide

    grown = expand(grown_t)
    weigh = expand(weights_t)
    s_step(8)
    sid = request_state[z]
    sid = jnp.where(sid < Z, sid, shared_id[0])
    j_state = (z - owner_map[sid] + Z) % Z
    prior = S[j_state]
    base = lax.dot_general(outv[...], prior, (((1,), (1,)), ((), ())), preferred_element_type=F32) * grown
    ext[0:8, :] = jnp.concatenate([jnp.zeros((5, CH), F32), M[j_state].astype(F32)[8:11]], axis=0)

    w_step(8)
    project(8)
    projected = acc[...].astype(BF).astype(F32)
    ext[8 : 8 + TOK, :] = projected
    ftail_ref[...] = ext[TOK + 5 : TOK + 8, :]
    conv = conv_b[...] + conv_w[0:1, :] * ext[5 : 5 + TOK, :]
    for k in range(1, 4):
        conv = conv + conv_w[k : k + 1, :] * ext[5 + k : 5 + k + TOK, :]
    conv_f = (conv / (1.0 + jnp.exp(-conv))).astype(BF).astype(F32)
    skip = jnp.zeros((1, CH), F32)
    one = lax.broadcasted_iota(jnp.int32, (1, CH), 1) // 64
    for h in range(HEADS):
        skip = jnp.where(one == h, skip_gain[h], skip)
        xbd[h] = jnp.where(chan == h, conv_f, 0.0).astype(BF)
    rest = base + skip * conv_f
    for tb in range(2):
        rows = pl.ds(256 * tb, 256)
        cols = 256 * (tb + 1)
        inner = rest[256 * tb : 256 * tb + 256]
        for h in range(HEADS):
            inner = inner + jnp.dot(mix[h, rows, 0:cols], xbd[h, 0:cols, :], preferred_element_type=F32)
        out_ref[rows, :] = inner.astype(BF)
    weighted = (conv_f * weigh).astype(BF)
    new_t = jnp.dot(inT[...], weighted, preferred_element_type=F32)
    head_row = lax.broadcasted_iota(jnp.int32, (CH, 1), 0) // 64
    kept = jnp.zeros((CH, 1), F32)
    last_e = jnp.exp(last)
    for h in range(HEADS):
        kept = jnp.where(head_row == h, last_e[h : h + 1, 0:1], kept)
    fstate_ref[...] = kept * prior.astype(F32) + new_t.T

    for copy in sends:
        copy.wait_send()


def on_device(
    layer_input, proj_weight, step_weight, step_bias, decay_log, conv_weight, conv_bias, skip_gain,
    group_inputs, cached_state, cached_tail, owner_map, request_state, shared_id,
):
    sw = step_weight.T.reshape(4, 2, 256).transpose(1, 0, 2).reshape(8, 256)
    misc = jnp.concatenate([sw, cached_tail[0].astype(BF), jnp.zeros((5, CH), BF)], axis=0)
    smem = pl.BlockSpec(memory_space=pltpu.SMEM)
    vmem = pl.BlockSpec(memory_space=pltpu.VMEM)
    hbm = pl.BlockSpec(memory_space=pl.ANY)
    dma = pltpu.SemaphoreType.DMA
    out, fstate, ftail = pl.pallas_call(
        body,
        out_shape=(
            jax.ShapeDtypeStruct((TOK, CH), BF),
            jax.ShapeDtypeStruct((CH, N), F32),
            jax.ShapeDtypeStruct((3, CH), F32),
        ),
        in_specs=[smem] * 6 + [hbm] * 5 + [vmem] * 2,
        out_specs=(vmem, vmem, vmem),
        scratch_shapes=[
            pltpu.VMEM((2, 2, 4, 4, 256, 256), BF),
            pltpu.VMEM((Z, 512, 256), BF),
            pltpu.VMEM((Z, 256, 256), BF),
            pltpu.VMEM((Z, 16, 256), BF),
            pltpu.VMEM((2, 4, 64, 512), BF),
            pltpu.VMEM((256, 256), F32),
            pltpu.VMEM((512, 64), BF),
            pltpu.VMEM((512, 256), F32),
            pltpu.VMEM((2, 16, 512), F32),
            pltpu.VMEM((8 + TOK, 256), F32),
            pltpu.VMEM((256, 512), BF),
            pltpu.VMEM((512, 256), BF),
            pltpu.VMEM((512, 512), F32),
            pltpu.VMEM((4, 512, 512), BF),
            pltpu.VMEM((4, 512, 256), BF),
            dma((6,)),
            dma((2, 8, WSUB)),
            dma((2, 8, WSUB)),
            dma((2, 8, SSUB)),
            dma((2, 8, SSUB)),
            dma((2, 8, 1)),
            dma((2, 8, 1)),
            dma((2, 2, 4)),
            dma((2, 2, 4)),
            dma((2, 4)),
            dma((2, 4)),
            dma((5,)),
            dma((5,)),
        ],
        compiler_params=pltpu.CompilerParams(
            collective_id=0, has_side_effects=True, vmem_limit_bytes=56 * 1024 * 1024
        ),
    )(
        request_state, owner_map, shared_id, step_bias, decay_log, skip_gain,
        layer_input, proj_weight, misc, cached_state.reshape(CH, N), group_inputs,
        conv_weight, conv_bias.reshape(1, CH),
    )
    return out, fstate.reshape(1, HEADS, 64, N), ftail[None]


def solution(mesh):
    return jax.shard_map(
        on_device,
        mesh=mesh,
        in_specs=(
            P("rep", "head"), P("rep", "head"), P("rep", "head"), P("head"), P("head"), P(None, "head"),
            P("head"), P("head"), P("rep", "head"), P("rep", "head", None, None), P("rep", None, "head"),
            P(), P(), P(),
        ),
        out_specs=(P("rep", "head"), P("rep", "head", None, None), P("rep", None, "head")),
        check_vma=False,
    )
```

```python
import functools

import jax
import jax.numpy as jnp
from jax import lax
from jax.experimental import pallas as pl
from jax.experimental.pallas import tpu as pltpu
from jax.sharding import PartitionSpec as P

MESH = pl.DeviceIdType.MESH
BF = jnp.bfloat16
F32 = jnp.float32
Z = 16
TOK = 512
CH = 256
HEADS = 4
N = 256
WSUB = 4
SSUB = 2
STEPS = 9
HELD = STEPS + 2
REACH = (9, 6)


def body(
    fast,
    request_state, owner_map, shared_id, step_bias, decay_log, skip_gain,
    x_hbm, w_hbm, sw_hbm, tail_hbm, state_hbm, g_hbm, conv_w, conv_b,
    out_ref, fstate_ref, ftail_ref, flag_ref,
    A, W, S, M, G, stage, landed, plan_v, plan, state_own, sw_own, tail_own, acc, sacc, ext, inT, outv, score, mix, xbd, rates, rate_t,
    loc_sem, ws_sem, wr_sem, ss_sem, sr_sem, ms_sem, mr_sem, as_sem, ar_sem, cs_sem, cr_sem, gs_sem, gr_sem, vs_sem, vr_sem, plan_sem,
):
    z = lax.axis_index("rep")
    hid = lax.axis_index("head")
    x, y, c = hid // 8, (hid // 2) % 4, hid % 2
    zr, zl = (z + 1) % Z, (z + Z - 1) % Z

    def dev(xx, yy, cc):
        return {"head": xx * 8 + yy * 2 + cc}

    xp, xm, yp, ym = (x + 1) % 4, (x + 3) % 4, (y + 1) % 4, (y + 3) % 4
    sibling = dev(x, y, 1 - c)
    zdev = ({"rep": zr}, {"rep": zl})
    pos = ((y, x), (x, y))
    x_nb, y_nb = (dev(xp, y, c), dev(xm, y, c)), (dev(x, yp, c), dev(x, ym, c))
    q_nb, p_nb = (x_nb, y_nb), (y_nb, x_nb)

    barrier = pltpu.get_barrier_semaphore()
    for d in (*zdev, *x_nb, *y_nb, sibling):
        pl.semaphore_signal(barrier, inc=1, device_id=d, device_id_type=MESH)

    locs = [
        pltpu.make_async_copy(sw_hbm, sw_own, loc_sem.at[0]),
        pltpu.make_async_copy(tail_hbm, tail_own, loc_sem.at[1]),
        pltpu.make_async_copy(state_hbm, state_own, loc_sem.at[2]),
        pltpu.make_async_copy(w_hbm, W.at[0], loc_sem.at[3]),
        pltpu.make_async_copy(x_hbm.at[0:256], A.at[0, c, y, x], loc_sem.at[4]),
        pltpu.make_async_copy(x_hbm.at[256:512], A.at[1, c, x, y], loc_sem.at[5]),
        pltpu.make_async_copy(g_hbm, G.at[c, y], loc_sem.at[6]),
    ]
    for copy in locs:
        copy.start()
    locs[0].wait()
    locs[1].wait()
    sw = sw_own[...].astype(F32)
    M[0] = jnp.concatenate(
        [sw[:, 0:256], sw[:, 256:512]] + [tail_own[k] for k in range(3)] + [jnp.zeros((5, CH), F32)], axis=0
    ).astype(BF)
    locs[2].wait()
    own = state_own[...].astype(BF)
    if fast:
        S[...] = jnp.zeros_like(S)
        for way in (0, 1):
            for part in (0, 1):
                S[way * HELD + part] = own[128 * part : 128 * part + 128]
    else:
        S[0] = own
    for i in range(3, 7):
        locs[i].wait()
    pl.semaphore_wait(barrier, 7)

    sends = []

    def rcopy(src, dst, s_sem, r_sem, d):
        return pltpu.make_async_remote_copy(
            src_ref=src, dst_ref=dst, send_sem=s_sem, recv_sem=r_sem, device_id=d, device_id_type=MESH
        )

    def go(ref, s_sem, r_sem, d, dst=None):
        copy = rcopy(ref, ref if dst is None else dst, s_sem, r_sem, d)
        copy.start()
        sends.append(copy)

    def got(ref, s_sem, r_sem, d):
        rcopy(ref, ref, s_sem, r_sem, d).wait_recv()

    def slot(way, s):
        return s if way == 0 else (Z - s) % Z

    def ring(buf, rows, sub, s_sem, r_sem, way, s):
        here = buf.at[slot(way, s), rows]
        if s > 0:
            got(here, s_sem.at[way, s - 1, sub], r_sem.at[way, s - 1, sub], zdev[way])
        if s < 8 and not (s == 7 and sub not in last_subs(way, s_sem)):
            go(here, s_sem.at[way, s, sub], r_sem.at[way, s, sub], zdev[way], buf.at[slot(way, s + 1), rows])

    def last_subs(way, s_sem):
        if s_sem is ws_sem:
            return (0, 1) if way == 0 else (2, 3)
        if s_sem is ss_sem:
            return (0,) if way == 0 else (1,)
        return (0,) if way == 0 else ()

    def w_step(s, subs=range(WSUB)):
        for sub in subs:
            for way in (0, 1):
                if s < 8 or sub in last_subs(way, ws_sem):
                    ring(W, pl.ds(sub * (512 // WSUB), 512 // WSUB), sub, ws_sem, wr_sem, way, s)

    def s_step(s, subs=range(SSUB)):
        for sub in subs:
            for way in (0, 1):
                if s < 8 or sub in last_subs(way, ss_sem):
                    ring(S, pl.ds(sub * (256 // SSUB), 256 // SSUB), sub, ss_sem, sr_sem, way, s)

    def state_row(q):
        sid = request_state[q]
        return owner_map[jnp.where(sid < Z, sid, shared_id[0])]

    def make_plan():
        pack = lax.broadcasted_iota(jnp.int32, (1, 64), 1)
        way, src, part = pack // 32, (pack % 32) // 2, pack % 2
        most = jnp.where(part == 0, REACH[0], REACH[1])
        togo = jnp.zeros((1, 64), jnp.int32)
        for q in range(Z):
            row = state_row(q)
            d = (q - row + Z) % Z
            ahead = jnp.where((d <= most) & (way == 0), d, 0)
            behind = jnp.where((d > most) & (way == 1), Z - d, 0)
            togo = jnp.maximum(togo, jnp.where(src == row, ahead + behind, 0))
        togo = togo.astype(F32)
        at = src
        name = (src * 2 + part + 1).astype(F32)
        code = (part + 1).astype(F32)
        order = pack.astype(F32)
        link_row = lax.broadcasted_iota(jnp.int32, (32, 64), 0)
        sent, came = [], []
        for t in range(STEPS):
            key = jnp.where(togo > 0.0, togo * 64.0 + order, 0.0)
            here = link_row == at + way * Z
            best = jnp.max(jnp.where(here, key, 0.0), axis=1, keepdims=True)
            wins = here & (key == best) & (key > 0.0)
            win = jnp.max(jnp.where(wins, 1.0, 0.0), axis=0, keepdims=True)
            then = jnp.where(way == 0, (at + 1) % Z, (at + Z - 1) % Z)
            sent.append(jnp.where(at == z, win * code, 0.0))
            came.append(jnp.where(then == z, win * name, 0.0))
            togo = togo - win
            code = jnp.where(win > 0.0, t + 3.0, code)
            at = jnp.where(win > 0.0, then, at)
        rest = [jnp.zeros((Z - STEPS, 64), F32)]
        sent, came = jnp.concatenate(sent + rest, axis=0), jnp.concatenate(came + rest, axis=0)
        half = lax.broadcasted_iota(jnp.int32, (Z, 64), 1) // 32
        lane = lax.broadcasted_iota(jnp.int32, (Z, 128), 1)
        table = jnp.zeros((Z, 128), F32)
        for k, (what, w) in enumerate(((sent, 0), (sent, 1), (came, 0), (came, 1))):
            column = jnp.max(jnp.where(half == w, what, 0.0), axis=1, keepdims=True)
            table = jnp.where(lane == k, column, table)
        table = jnp.where(lane == 4, jnp.max(togo, axis=1, keepdims=True), table)
        plan_v[...] = table.astype(jnp.int32)
        copy = pltpu.make_async_copy(plan_v, plan, plan_sem)
        copy.start()
        copy.wait()
        flag_ref[0] = plan[0, 4]

    def convey(t):
        for way in (0, 1):
            if t > 0:
                got(landed.at[way, t - 1], vs_sem.at[way, t - 1], vr_sem.at[way, t - 1], zdev[way])
                S[way * HELD + t + 1] = landed[way, t - 1]
            if t < STEPS:
                k = jnp.clip(plan[t, way] - 1, 0, HELD - 1)
                stage[way, t] = S[way * HELD + k]
                go(stage.at[way, t], vs_sem.at[way, t], vr_sem.at[way, t], zdev[way], landed.at[way, t])

    def prior_half(row, part):
        at = part
        for way in (0, 1):
            for t in range(STEPS):
                at = jnp.where(plan[t, 2 + way] == row * 2 + part + 1, way * HELD + t + 2, at)
        return S[at]

    def m_step(s):
        for way in (0, 1):
            if s < 8 or 0 in last_subs(way, ms_sem):
                ring(M, pl.ds(0, 16), 0, ms_sem, mr_sem, way, s)

    def ring4(stage, blk, halves, nb, s_sem, r_sem):
        if stage == 0:
            for way in (0, 1):
                go(blk(0), s_sem.at[way], r_sem.at[way], nb[way])
        elif stage == 1:
            for way, step in ((0, -1), (1, 1)):
                got(blk(step), s_sem.at[way], r_sem.at[way], nb[way])
                go(halves(blk(step), way), s_sem.at[2 + way], r_sem.at[2 + way], nb[way])
        else:
            for way in (0, 1):
                got(halves(blk(2), way), s_sem.at[2 + way], r_sem.at[2 + way], nb[way])

    def a_one(stage, i):
        p, q = pos[i]
        ring4(
            stage,
            lambda k: A.at[i, c, p, (q + 4 + k) % 4],
            lambda ref, way: ref.at[pl.ds(128 * way, 128)],
            q_nb[i], as_sem.at[i, 0], ar_sem.at[i, 0],
        )

    def a_two(stage, i):
        p, _ = pos[i]

        def part(k, piece):
            return A.at[i, c, (p + 4 + k) % 4, pl.ds(2 * piece, 2)]

        def sems(n, way):
            return as_sem.at[i, 1 + n, way], ar_sem.at[i, 1 + n, way]

        for way, step in ((0, -1), (1, 1)):
            d = p_nb[i][way]
            if stage == 0:
                go(part(0, way), *sems(0, way), d)
                go(part(0, 1 - way), *sems(1, way), d)
            elif stage == 1:
                got(part(step, way), *sems(0, way), d)
                go(part(step, way), *sems(2, way), d)
            elif stage == 2:
                got(part(step, 1 - way), *sems(1, way), d)
            else:
                got(part(2, way), *sems(2, way), d)

    def a_share(i, k):
        p, _ = pos[i]
        go(A.at[i, c, (p + k) % 4], cs_sem.at[i, k], cr_sem.at[i, k], sibling)

    def a_shared(i, k):
        p, _ = pos[i]
        got(A.at[i, 1 - c, (p + k) % 4], cs_sem.at[i, k], cr_sem.at[i, k], sibling)

    def g_ring(stage):
        ring4(
            stage,
            lambda k: G.at[c, (y + 4 + k) % 4],
            lambda ref, way: ref.at[pl.ds(32 * way, 32)],
            y_nb, gs_sem, gr_sem,
        )

    def a_block(i, kz, cc):
        ax, ay = kz // 4, kz % 4
        return A[0, cc, ay, ax] if i == 0 else A[1, cc, ax, ay]

    def project(j):
        kz = (z - j + Z) % Z
        for i in (0, 1):
            rows = pl.ds(256 * i, 256)
            part = jnp.dot(a_block(i, kz, 0), W[j, 0:256], preferred_element_type=F32)
            part += jnp.dot(a_block(i, kz, 1), W[j, 256:512], preferred_element_type=F32)
            acc[rows, :] += part

    def step_part(j):
        kz = (z - j + Z) % Z
        for i in (0, 1):
            for cc in (0, 1):
                sacc[cc, :, pl.ds(256 * i, 256)] += lax.dot_general(
                    M[j], a_block(i, kz, cc), (((1,), (1,)), ((), ())), preferred_element_type=F32
                )

    def vectors():
        for k in range(4):
            inT[pl.ds(64 * k, 64), :] = G[k % 2, k // 2]
            outv[:, pl.ds(64 * k, 64)] = G[k % 2, 2 + k // 2].astype(F32).T.astype(BF)

    def scores(tb):
        t0 = tb * 128
        cols = 256 if tb < 2 else 512
        sc = jnp.dot(outv[pl.ds(t0, 128), :], inT[:, 0:cols], preferred_element_type=F32)
        keep = lax.broadcasted_iota(jnp.int32, (128, cols), 1) <= t0 + lax.broadcasted_iota(jnp.int32, (128, cols), 0)
        score[pl.ds(t0, 128), 0:cols] = jnp.where(keep, sc, 0.0)

    def decays():
        row = lax.broadcasted_iota(jnp.int32, (8, 1), 0)

        def per_head(ref):
            col = jnp.zeros((8, 1), F32)
            for h in range(HEADS):
                col = jnp.where(row == h, ref[h], col)
            return col

        raw = jnp.concatenate([sacc[0, 0:4] + sacc[1, 4:8], jnp.zeros((4, TOK), F32)], axis=0)
        raw = raw + per_head(step_bias)
        step = jnp.maximum(raw, 0.0) + jnp.log1p(jnp.exp(-jnp.abs(raw)))
        decay = -jnp.exp(per_head(decay_log)) * step
        lane = lax.broadcasted_iota(jnp.int32, (8, TOK), 1)
        for k in range(9):
            decay = decay + jnp.where(lane >= 2**k, pltpu.roll(decay, 2**k, axis=1), 0.0)
        last = decay[:, TOK - 1 : TOK]
        weights = jnp.exp(last - decay) * step
        rates[0] = decay
        rates[1] = step
        decay_t = jnp.concatenate([decay, jnp.zeros((120, TOK), F32)], axis=0).T
        grown_t = jnp.exp(decay_t)
        weights_t = jnp.concatenate([weights, jnp.zeros((120, TOK), F32)], axis=0).T
        rate_t[0] = decay_t
        rate_t[1] = grown_t
        rate_t[2] = weights_t

    def make_mix(h):
        for tb in range(4):
            t0 = tb * 128
            cols = 256 if tb < 2 else 512
            differ = rate_t[0, t0 : t0 + 128, h : h + 1] - rates[0, h : h + 1, 0:cols]
            scaled = jnp.exp(jnp.minimum(differ, 0.0)) * rates[1, h : h + 1, 0:cols]
            mix[h, pl.ds(t0, 128), 0:cols] = (score[pl.ds(t0, 128), 0:cols] * scaled).astype(BF)

    def step_parts(first):
        @pl.loop(first, first + 4)
        def _(j):
            step_part(j)

    def projects(first, end):
        @pl.loop(first, end)
        def _(j):
            project(j)
            project(Z - j)

    def g_share():
        go(G.at[c], gs_sem.at[4], gr_sem.at[4], sibling)

    def g_shared():
        got(G.at[1 - c], gs_sem.at[4], gr_sem.at[4], sibling)

    def both(f, *args):
        for i in (0, 1):
            f(*args, i)

    def shared(i):
        for k in range(4):
            a_shared(i, k)

    def clear():
        acc[...] = jnp.zeros_like(acc)
        sacc[...] = jnp.zeros_like(sacc)

    work = {u: [] for u in range(4 * 9)}

    def add(u, f, *args):
        work[u].append((f, args))

    if fast:
        for t in range(1, STEPS + 1):
            add(2 + 31 * t // STEPS, convey, t)
    else:
        for s in range(1, 9):
            add(4 * s, s_step, s)
    for s, u in enumerate((0, 4, 6, 8, 10, 13, 15, 18, 20)):
        if s:
            add(u, m_step, s)
    add(3, clear)
    add(5, both, a_one, 1)
    add(5, g_ring, 1)
    add(7, g_ring, 2)
    add(7, g_share)
    add(8, both, a_one, 2)
    add(8, both, a_two, 0)
    add(8, lambda: both(lambda i: a_share(i, 0)))
    add(11, g_shared)
    add(11, vectors)
    add(13, both, a_two, 1)
    for tb in range(4):
        add(12 + tb, scores, tb)
    add(16, both, a_two, 2)
    add(16, lambda: both(lambda i: (a_share(i, 3), a_share(i, 1))))
    add(19, both, a_two, 3)
    add(19, lambda: both(lambda i: a_share(i, 2)))
    add(21, both, shared)
    for k in range(4):
        add(21 + k, step_parts, 4 * k)
    add(24, decays)
    for h in range(HEADS):
        add(25 + h, make_mix, h)
    add(28, project, 0)
    add(29, projects, 1, 3)
    add(30, projects, 3, 5)
    add(31, projects, 5, 7)
    add(32, projects, 7, 8)

    m_step(0)
    both(a_one, 0)
    w_step(0, (0, 1))
    if fast:
        make_plan()
        convey(0)
    else:
        s_step(0)
    w_step(0, (2, 3))
    g_ring(0)
    for u in range(3, 36):
        if u > 3:
            w_step(u // 4, (u % 4,))
        for f, args in work[u]:
            f(*args)

    chan = lax.broadcasted_iota(jnp.int32, (TOK, CH), 1) // 64

    def expand(cols):
        wide = jnp.broadcast_to(cols[:, 0:1], (TOK, CH))
        for h in range(1, HEADS):
            wide = jnp.where(chan == h, cols[:, h : h + 1], wide)
        return wide

    grown = expand(rate_t[1])
    weigh = expand(rate_t[2])
    row = state_row(z)
    j_state = (z - row + Z) % Z
    if fast:
        prior = jnp.concatenate([prior_half(row, 0), prior_half(row, 1)], axis=0)
    else:
        prior = S[j_state]
    base = lax.dot_general(outv[...], prior, (((1,), (1,)), ((), ())), preferred_element_type=F32) * grown
    ext[0:8, :] = jnp.concatenate([jnp.zeros((5, CH), F32), M[j_state].astype(F32)[8:11]], axis=0)

    project(8)
    projected = acc[...].astype(BF).astype(F32)
    ext[8 : 8 + TOK, :] = projected
    for k in range(3):
        ftail_ref[k] = ext[TOK + 5 + k : TOK + 6 + k, :]
    conv = conv_b[...] + conv_w[0:1, :] * ext[5 : 5 + TOK, :]
    for k in range(1, 4):
        conv = conv + conv_w[k : k + 1, :] * ext[5 + k : 5 + k + TOK, :]
    conv_f = (conv / (1.0 + jnp.exp(-conv))).astype(BF).astype(F32)
    skip = jnp.zeros((1, CH), F32)
    one = lax.broadcasted_iota(jnp.int32, (1, CH), 1) // 64
    for h in range(HEADS):
        skip = jnp.where(one == h, skip_gain[h], skip)
        xbd[h] = jnp.where(chan == h, conv_f, 0.0).astype(BF)
    rest = base + skip * conv_f
    for tb in range(2):
        rows = pl.ds(256 * tb, 256)
        cols = 256 * (tb + 1)
        inner = rest[256 * tb : 256 * tb + 256]
        for h in range(HEADS):
            inner = inner + jnp.dot(mix[h, rows, 0:cols], xbd[h, 0:cols, :], preferred_element_type=F32)
        out_ref[rows, :] = inner.astype(BF)
    weighted = (conv_f * weigh).astype(BF)
    new_t = jnp.dot(inT[...], weighted, preferred_element_type=F32)
    head_row = lax.broadcasted_iota(jnp.int32, (CH, 1), 0) // 64
    kept = jnp.zeros((CH, 1), F32)
    last_e = jnp.exp(rates[0, :, TOK - 1 : TOK])
    for h in range(HEADS):
        kept = jnp.where(head_row == h, last_e[h : h + 1, 0:1], kept)
    fstate_ref[...] = kept * prior.astype(F32) + new_t.T

    for copy in sends:
        copy.wait_send()
    if not fast:
        flag_ref[0] = 0


def put(*refs):
    srcs, dsts, mids, sem = refs[0:3], refs[3:6], refs[6:9], refs[9]
    gets = [pltpu.make_async_copy(src, mid, sem.at[k]) for k, (src, mid) in enumerate(zip(srcs, mids))]
    puts = [pltpu.make_async_copy(mid, dst, sem.at[3 + k]) for k, (mid, dst) in enumerate(zip(mids, dsts))]
    for get in gets:
        get.start()
    for get, one in zip(gets, puts):
        get.wait()
        one.start()
    for one in puts:
        one.wait()


def on_device(
    layer_input, proj_weight, step_weight, step_bias, decay_log, conv_weight, conv_bias, skip_gain,
    group_inputs, cached_state, cached_tail, owner_map, request_state, shared_id,
):
    smem = pl.BlockSpec(memory_space=pltpu.SMEM)
    vmem = pl.BlockSpec(memory_space=pltpu.VMEM)
    hbm = pl.BlockSpec(memory_space=pl.ANY)
    dma = pltpu.SemaphoreType.DMA
    shapes = (
        jax.ShapeDtypeStruct((TOK, CH), BF),
        jax.ShapeDtypeStruct((CH, N), F32),
        jax.ShapeDtypeStruct((3, 1, CH), F32),
    )
    args = (
        request_state, owner_map, shared_id, step_bias, decay_log, skip_gain,
        layer_input, proj_weight, step_weight.T, cached_tail.transpose(1, 0, 2), cached_state.reshape(CH, N), group_inputs.T,
        conv_weight, conv_bias.reshape(1, CH),
    )

    def layer(fast):
        return pl.pallas_call(
            functools.partial(body, fast),
            out_shape=(*shapes, jax.ShapeDtypeStruct((1,), jnp.int32)),
            in_specs=[smem] * 6 + [hbm] * 6 + [vmem] * 2,
            out_specs=(vmem, vmem, vmem, smem),
            scratch_shapes=[
                pltpu.VMEM((2, 2, 4, 4, 256, 256), BF),
                pltpu.VMEM((Z, 512, 256), BF),
                pltpu.VMEM((2 * HELD, 128, 256) if fast else (Z, 256, 256), BF),
                pltpu.VMEM((Z, 16, 256), BF),
                pltpu.VMEM((2, 4, 64, 512), BF),
                pltpu.VMEM((2, STEPS, 128, 256), BF),
                pltpu.VMEM((2, STEPS, 128, 256), BF),
                pltpu.VMEM((Z, 128), jnp.int32),
                pltpu.SMEM((Z, 128), jnp.int32),
                pltpu.VMEM((256, 256), F32),
                pltpu.VMEM((4, 512), BF),
                pltpu.VMEM((3, 1, 256), F32),
                pltpu.VMEM((512, 256), F32),
                pltpu.VMEM((2, 16, 512), F32),
                pltpu.VMEM((8 + TOK, 256), F32),
                pltpu.VMEM((256, 512), BF),
                pltpu.VMEM((512, 256), BF),
                pltpu.VMEM((512, 512), F32),
                pltpu.VMEM((4, 512, 512), BF),
                pltpu.VMEM((4, 512, 256), BF),
                pltpu.VMEM((2, 8, 512), F32),
                pltpu.VMEM((3, 512, 128), F32),
                dma((7,)),
                dma((2, 8, WSUB)),
                dma((2, 8, WSUB)),
                dma((2, 8, SSUB)),
                dma((2, 8, SSUB)),
                dma((2, 8, 1)),
                dma((2, 8, 1)),
                dma((2, 4, 4)),
                dma((2, 4, 4)),
                dma((2, 4)),
                dma((2, 4)),
                dma((5,)),
                dma((5,)),
                dma((2, STEPS)),
                dma((2, STEPS)),
                dma,
            ],
            compiler_params=pltpu.CompilerParams(
                collective_id=0 if fast else 1, has_side_effects=True, vmem_limit_bytes=56 * 1024 * 1024
            ),
        )(*args)

    *results, left = layer(True)

    def place(*values):
        return pl.pallas_call(
            put,
            out_shape=shapes,
            in_specs=[hbm] * 3,
            out_specs=[hbm] * 3,
            scratch_shapes=[pltpu.VMEM(v.shape, v.dtype) for v in shapes] + [dma((6,))],
            compiler_params=pltpu.CompilerParams(vmem_limit_bytes=60 * 1024 * 1024),
        )(*values)

    def again(*_):
        return tuple(layer(False)[0:3])

    out, fstate, ftail = lax.cond(left[0] == 0, place, again, *results)
    return out, fstate.reshape(1, HEADS, 64, N), ftail.transpose(1, 0, 2)


def solution(mesh):
    return jax.shard_map(
        on_device,
        mesh=mesh,
        in_specs=(
            P("rep", "head"), P("rep", "head"), P("rep", "head"), P("head"), P("head"), P(None, "head"),
            P("head"), P("head"), P("rep", "head"), P("rep", "head", None, None), P("rep", None, "head"),
            P(), P(), P(),
        ),
        out_specs=(P("rep", "head"), P("rep", "head", None, None), P("rep", None, "head")),
        check_vma=False,
    )
```

```python
import jax
import jax.numpy as jnp
from jax import lax
from jax.experimental import pallas as pl
from jax.experimental.pallas import tpu as pltpu
from jax.sharding import PartitionSpec as P

MESH = pl.DeviceIdType.MESH
BF = jnp.bfloat16
F32 = jnp.float32
Z = 16
TOK = 512
CH = 256
HEADS = 4
N = 256
WSUB = 4
STEPS = 10
HELD = STEPS + 2
REACH = (10, 5)


def body(
    request_state, owner_map, shared_id, step_bias, decay_log, skip_gain,
    x_hbm, w_hbm, sw_hbm, tail_hbm, state_hbm, g_hbm, conv_w, conv_b,
    out_ref, fstate_ref, ftail_ref,
    A, W, S, M, G, stage, landed, plan_v, plan, state_own, sw_own, tail_own, acc, sacc, ext, inT, outv, score, mix, xbd, rates, rate_t, base, weigh, carry,
    loc_sem, ws_sem, wr_sem, ms_sem, mr_sem, as_sem, ar_sem, cs_sem, cr_sem, gs_sem, gr_sem, vs_sem, vr_sem, plan_sem,
):
    z = lax.axis_index("rep")
    hid = lax.axis_index("head")
    x, y, c = hid // 8, (hid // 2) % 4, hid % 2
    zr, zl = (z + 1) % Z, (z + Z - 1) % Z

    def dev(xx, yy, cc):
        return {"head": xx * 8 + yy * 2 + cc}

    xp, xm, yp, ym = (x + 1) % 4, (x + 3) % 4, (y + 1) % 4, (y + 3) % 4
    sibling = dev(x, y, 1 - c)
    zdev = ({"rep": zr}, {"rep": zl})
    pos = ((y, x), (x, y))
    x_nb, y_nb = (dev(xp, y, c), dev(xm, y, c)), (dev(x, yp, c), dev(x, ym, c))
    q_nb, p_nb = (x_nb, y_nb), (y_nb, x_nb)

    barrier = pltpu.get_barrier_semaphore()
    for d in (*zdev, *x_nb, *y_nb, sibling):
        pl.semaphore_signal(barrier, inc=1, device_id=d, device_id_type=MESH)

    sends = []

    def rcopy(src, dst, s_sem, r_sem, d):
        return pltpu.make_async_remote_copy(
            src_ref=src, dst_ref=dst, send_sem=s_sem, recv_sem=r_sem, device_id=d, device_id_type=MESH
        )

    def go(ref, s_sem, r_sem, d, dst=None):
        copy = rcopy(ref, ref if dst is None else dst, s_sem, r_sem, d)
        copy.start()
        sends.append(copy)

    def got(ref, s_sem, r_sem, d):
        rcopy(ref, ref, s_sem, r_sem, d).wait_recv()

    def slot(way, s):
        return s if way == 0 else (Z - s) % Z

    def ring(buf, rows, sub, s_sem, r_sem, way, s):
        here = buf.at[slot(way, s), rows]
        if s > 0:
            got(here, s_sem.at[way, s - 1, sub], r_sem.at[way, s - 1, sub], zdev[way])
        if s < 8 and not (s == 7 and sub not in last_subs(way, s_sem)):
            go(here, s_sem.at[way, s, sub], r_sem.at[way, s, sub], zdev[way], buf.at[slot(way, s + 1), rows])

    def last_subs(way, s_sem):
        if s_sem is ws_sem:
            return (0, 1) if way == 0 else (2, 3)
        return (0,) if way == 0 else ()

    def w_step(s, subs=range(WSUB)):
        for sub in subs:
            for way in (0, 1):
                if s < 8 or sub in last_subs(way, ws_sem):
                    ring(W, pl.ds(sub * (512 // WSUB), 512 // WSUB), sub, ws_sem, wr_sem, way, s)

    def early():
        pl.semaphore_wait(barrier, 7)
        for sub in (0, 1):
            rows = pl.ds(128 * sub, 128)
            for way in (0, 1):
                go(w_hbm.at[rows], ws_sem.at[way, 0, sub], wr_sem.at[way, 0, sub], zdev[way], W.at[slot(way, 1), rows])

    locs = [
        pltpu.make_async_copy(sw_hbm, sw_own, loc_sem.at[0]),
        pltpu.make_async_copy(tail_hbm, tail_own, loc_sem.at[1]),
        pltpu.make_async_copy(state_hbm, state_own, loc_sem.at[2]),
        pltpu.make_async_copy(w_hbm, W.at[0], loc_sem.at[3]),
        pltpu.make_async_copy(x_hbm.at[0:256], A.at[0, c, y, x], loc_sem.at[4]),
        pltpu.make_async_copy(x_hbm.at[256:512], A.at[1, c, x, y], loc_sem.at[5]),
        pltpu.make_async_copy(g_hbm, G.at[c, y], loc_sem.at[6]),
    ]
    for copy in locs:
        copy.start()
    early()
    locs[0].wait()
    locs[1].wait()
    sw = sw_own[...].astype(F32)
    M[0] = jnp.concatenate(
        [sw[:, 0:256], sw[:, 256:512]] + [tail_own[k] for k in range(3)] + [jnp.zeros((5, CH), F32)], axis=0
    ).astype(BF)
    locs[2].wait()
    own = state_own[...].astype(BF)
    S[...] = jnp.zeros_like(S)
    for way in (0, 1):
        for part in (0, 1):
            S[way * HELD + part] = own[128 * part : 128 * part + 128]
    for i in range(3, 7):
        locs[i].wait()

    def state_row(q):
        sid = request_state[q]
        return owner_map[jnp.where(sid < Z, sid, shared_id[0])]

    def make_plan():
        pack = lax.broadcasted_iota(jnp.int32, (1, 64), 1)
        way, src, part = pack // 32, (pack % 32) // 2, pack % 2
        most = jnp.where(part == 0, REACH[0], REACH[1])
        togo = jnp.zeros((1, 64), jnp.int32)
        for q in range(Z):
            row = state_row(q)
            d = (q - row + Z) % Z
            ahead = jnp.where((d <= most) & (way == 0), d, 0)
            behind = jnp.where((d > most) & (way == 1), Z - d, 0)
            togo = jnp.maximum(togo, jnp.where(src == row, ahead + behind, 0))
        togo = togo.astype(F32)
        at = src
        name = (src * 2 + part + 1).astype(F32)
        code = (part + 1).astype(F32)
        order = pack.astype(F32)
        link_row = lax.broadcasted_iota(jnp.int32, (32, 64), 0)
        sent, came = [], []
        for t in range(STEPS):
            key = jnp.where(togo > 0.0, togo * 64.0 + order, 0.0)
            here = link_row == at + way * Z
            best = jnp.max(jnp.where(here, key, 0.0), axis=1, keepdims=True)
            wins = here & (key == best) & (key > 0.0)
            win = jnp.max(jnp.where(wins, 1.0, 0.0), axis=0, keepdims=True)
            then = jnp.where(way == 0, (at + 1) % Z, (at + Z - 1) % Z)
            sent.append(jnp.where(at == z, win * code, 0.0))
            came.append(jnp.where(then == z, win * name, 0.0))
            togo = togo - win
            code = jnp.where(win > 0.0, t + 3.0, code)
            at = jnp.where(win > 0.0, then, at)
        rest = [jnp.zeros((Z - STEPS, 64), F32)]
        sent, came = jnp.concatenate(sent + rest, axis=0), jnp.concatenate(came + rest, axis=0)
        half = lax.broadcasted_iota(jnp.int32, (Z, 64), 1) // 32
        lane = lax.broadcasted_iota(jnp.int32, (Z, 128), 1)
        table = jnp.zeros((Z, 128), F32)
        for k, (what, w) in enumerate(((sent, 0), (sent, 1), (came, 0), (came, 1))):
            column = jnp.max(jnp.where(half == w, what, 0.0), axis=1, keepdims=True)
            table = jnp.where(lane == k, column, table)
        plan_v[...] = table.astype(jnp.int32)
        copy = pltpu.make_async_copy(plan_v, plan, plan_sem)
        copy.start()
        copy.wait()

    def convey(t):
        for way in (0, 1):
            if t > 0:
                got(landed.at[way, t - 1], vs_sem.at[way, t - 1], vr_sem.at[way, t - 1], zdev[way])
                S[way * HELD + t + 1] = landed[way, t - 1]
            if t < STEPS:
                k = jnp.clip(plan[t, way] - 1, 0, HELD - 1)
                stage[way, t] = S[way * HELD + k]
                go(stage.at[way, t], vs_sem.at[way, t], vr_sem.at[way, t], zdev[way], landed.at[way, t])

    def prior_half(row, part):
        at = part
        for way in (0, 1):
            for t in range(STEPS):
                at = jnp.where(plan[t, 2 + way] == row * 2 + part + 1, way * HELD + t + 2, at)
        return S[at]

    def m_step(s):
        for way in (0, 1):
            if s < 8 or 0 in last_subs(way, ms_sem):
                ring(M, pl.ds(0, 16), 0, ms_sem, mr_sem, way, s)

    def ring4(stage, blk, halves, nb, s_sem, r_sem):
        if stage == 0:
            for way in (0, 1):
                go(blk(0), s_sem.at[way], r_sem.at[way], nb[way])
        elif stage == 1:
            for way, step in ((0, -1), (1, 1)):
                got(blk(step), s_sem.at[way], r_sem.at[way], nb[way])
                go(halves(blk(step), way), s_sem.at[2 + way], r_sem.at[2 + way], nb[way])
        else:
            for way in (0, 1):
                got(halves(blk(2), way), s_sem.at[2 + way], r_sem.at[2 + way], nb[way])

    def a_one(stage, i):
        p, q = pos[i]
        ring4(
            stage,
            lambda k: A.at[i, c, p, (q + 4 + k) % 4],
            lambda ref, way: ref.at[pl.ds(128 * way, 128)],
            q_nb[i], as_sem.at[i, 0], ar_sem.at[i, 0],
        )

    def a_two(stage, i):
        p, _ = pos[i]

        def part(k, piece):
            return A.at[i, c, (p + 4 + k) % 4, pl.ds(2 * piece, 2)]

        def sems(n, way):
            return as_sem.at[i, 1 + n, way], ar_sem.at[i, 1 + n, way]

        for way, step in ((0, -1), (1, 1)):
            d = p_nb[i][way]
            if stage == 0:
                go(part(0, way), *sems(0, way), d)
                go(part(0, 1 - way), *sems(1, way), d)
            elif stage == 1:
                got(part(step, way), *sems(0, way), d)
                go(part(step, way), *sems(2, way), d)
            elif stage == 2:
                got(part(step, 1 - way), *sems(1, way), d)
            else:
                got(part(2, way), *sems(2, way), d)

    def a_share(i, k):
        p, _ = pos[i]
        go(A.at[i, c, (p + k) % 4], cs_sem.at[i, k], cr_sem.at[i, k], sibling)

    def a_shared(i, k):
        p, _ = pos[i]
        got(A.at[i, 1 - c, (p + k) % 4], cs_sem.at[i, k], cr_sem.at[i, k], sibling)

    def g_ring(stage):
        ring4(
            stage,
            lambda k: G.at[c, (y + 4 + k) % 4],
            lambda ref, way: ref.at[pl.ds(32 * way, 32)],
            y_nb, gs_sem, gr_sem,
        )

    def a_block(i, kz, cc):
        ax, ay = kz // 4, kz % 4
        return A[0, cc, ay, ax] if i == 0 else A[1, cc, ax, ay]

    def project(j):
        kz = (z - j + Z) % Z
        for i in (0, 1):
            rows = pl.ds(256 * i, 256)
            part = jnp.dot(a_block(i, kz, 0), W[j, 0:256], preferred_element_type=F32)
            part += jnp.dot(a_block(i, kz, 1), W[j, 256:512], preferred_element_type=F32)
            acc[rows, :] += part

    def step_part(j):
        kz = (z - j + Z) % Z
        for i in (0, 1):
            for cc in (0, 1):
                sacc[cc, :, pl.ds(256 * i, 256)] += lax.dot_general(
                    M[j], a_block(i, kz, cc), (((1,), (1,)), ((), ())), preferred_element_type=F32
                )

    def vectors():
        for k in range(4):
            inT[pl.ds(64 * k, 64), :] = G[k % 2, k // 2]
            outv[:, pl.ds(64 * k, 64)] = G[k % 2, 2 + k // 2].astype(F32).T.astype(BF)

    def scores(tb):
        t0 = tb * 128
        cols = 256 if tb < 2 else 512
        sc = jnp.dot(outv[pl.ds(t0, 128), :], inT[:, 0:cols], preferred_element_type=F32)
        keep = lax.broadcasted_iota(jnp.int32, (128, cols), 1) <= t0 + lax.broadcasted_iota(jnp.int32, (128, cols), 0)
        score[pl.ds(t0, 128), 0:cols] = jnp.where(keep, sc, 0.0)

    def decays():
        row = lax.broadcasted_iota(jnp.int32, (8, 1), 0)

        def per_head(ref):
            col = jnp.zeros((8, 1), F32)
            for h in range(HEADS):
                col = jnp.where(row == h, ref[h], col)
            return col

        raw = jnp.concatenate([sacc[0, 0:4] + sacc[1, 4:8], jnp.zeros((4, TOK), F32)], axis=0)
        raw = raw + per_head(step_bias)
        step = jnp.maximum(raw, 0.0) + jnp.log1p(jnp.exp(-jnp.abs(raw)))
        decay = -jnp.exp(per_head(decay_log)) * step
        lane = lax.broadcasted_iota(jnp.int32, (8, TOK), 1)
        for k in range(9):
            decay = decay + jnp.where(lane >= 2**k, pltpu.roll(decay, 2**k, axis=1), 0.0)
        last = decay[:, TOK - 1 : TOK]
        weights = jnp.exp(last - decay) * step
        rates[0] = decay
        rates[1] = step
        decay_t = jnp.concatenate([decay, jnp.zeros((120, TOK), F32)], axis=0).T
        grown_t = jnp.exp(decay_t)
        weights_t = jnp.concatenate([weights, jnp.zeros((120, TOK), F32)], axis=0).T
        rate_t[0] = decay_t
        rate_t[1] = grown_t
        rate_t[2] = weights_t

    def make_mix(h):
        for tb in range(4):
            t0 = tb * 128
            cols = 256 if tb < 2 else 512
            differ = rate_t[0, t0 : t0 + 128, h : h + 1] - rates[0, h : h + 1, 0:cols]
            scaled = jnp.exp(jnp.minimum(differ, 0.0)) * rates[1, h : h + 1, 0:cols]
            mix[h, pl.ds(t0, 128), 0:cols] = (score[pl.ds(t0, 128), 0:cols] * scaled).astype(BF)

    def step_parts(first):
        @pl.loop(first, first + 4)
        def _(j):
            step_part(j)

    def projects(first, end):
        @pl.loop(first, end)
        def _(j):
            project(j)
            project(Z - j)

    def g_share():
        go(G.at[c], gs_sem.at[4], gr_sem.at[4], sibling)

    def g_shared():
        got(G.at[1 - c], gs_sem.at[4], gr_sem.at[4], sibling)

    def both(f, *args):
        for i in (0, 1):
            f(*args, i)

    def shared(i):
        for k in range(4):
            a_shared(i, k)

    chan = lax.broadcasted_iota(jnp.int32, (TOK, CH), 1) // 64

    def clear():
        acc[...] = jnp.zeros_like(acc)
        sacc[...] = jnp.zeros_like(sacc)

    def expand(cols):
        wide = jnp.broadcast_to(cols[:, 0:1], (TOK, CH))
        for h in range(1, HEADS):
            wide = jnp.where(chan == h, cols[:, h : h + 1], wide)
        return wide

    def expand_decays():
        base[...] = expand(rate_t[1])
        weigh[...] = expand(rate_t[2])

    def resume():
        row = state_row(z)
        j_state = (z - row + Z) % Z
        prior = jnp.concatenate([prior_half(row, 0), prior_half(row, 1)], axis=0)
        base[...] *= lax.dot_general(outv[...], prior, (((1,), (1,)), ((), ())), preferred_element_type=F32)
        ext[0:8, :] = jnp.concatenate([jnp.zeros((5, CH), F32), M[j_state].astype(F32)[8:11]], axis=0)
        head_row = lax.broadcasted_iota(jnp.int32, (CH, 1), 0) // 64
        kept = jnp.zeros((CH, 1), F32)
        last_e = jnp.exp(rates[0, :, TOK - 1 : TOK])
        for h in range(HEADS):
            kept = jnp.where(head_row == h, last_e[h : h + 1, 0:1], kept)
        carry[...] = kept * prior.astype(F32)

    work = {u: [] for u in range(4 * 9)}

    def add(u, f, *args):
        work[u].append((f, args))

    for t in range(1, STEPS + 1):
        add(2 + 30 * t // STEPS, convey, t)
    for s, u in enumerate((0, 4, 6, 8, 10, 13, 15, 18, 20)):
        if s:
            add(u, m_step, s)
    add(3, clear)
    add(5, both, a_one, 1)
    add(5, g_ring, 1)
    add(7, g_ring, 2)
    add(7, g_share)
    add(8, both, a_one, 2)
    add(8, both, a_two, 0)
    add(8, lambda: both(lambda i: a_share(i, 0)))
    add(11, g_shared)
    add(11, vectors)
    add(13, both, a_two, 1)
    for tb in range(4):
        add(12 + tb, scores, tb)
    add(16, both, a_two, 2)
    add(16, lambda: both(lambda i: (a_share(i, 3), a_share(i, 1))))
    add(19, both, a_two, 3)
    add(19, lambda: both(lambda i: a_share(i, 2)))
    add(21, both, shared)
    for k in range(4):
        add(21 + k, step_parts, 4 * k)
    add(24, decays)
    for h in range(HEADS):
        add(25 + h, make_mix, h)
    add(28, expand_decays)
    add(28, project, 0)
    add(29, projects, 1, 3)
    add(30, projects, 3, 5)
    add(31, projects, 5, 7)
    add(32, projects, 7, 8)
    add(32, resume)

    m_step(0)
    both(a_one, 0)
    make_plan()
    convey(0)
    w_step(0, (2, 3))
    g_ring(0)
    for u in range(3, 36):
        if u > 3:
            w_step(u // 4, (u % 4,))
        for f, args in work[u]:
            f(*args)

    project(8)
    projected = acc[...].astype(BF).astype(F32)
    ext[8 : 8 + TOK, :] = projected
    for k in range(3):
        ftail_ref[k] = ext[TOK + 5 + k : TOK + 6 + k, :]
    conv = conv_b[...] + conv_w[0:1, :] * ext[5 : 5 + TOK, :]
    for k in range(1, 4):
        conv = conv + conv_w[k : k + 1, :] * ext[5 + k : 5 + k + TOK, :]
    conv_f = (conv / (1.0 + jnp.exp(-conv))).astype(BF).astype(F32)
    skip = jnp.zeros((1, CH), F32)
    one = lax.broadcasted_iota(jnp.int32, (1, CH), 1) // 64
    for h in range(HEADS):
        skip = jnp.where(one == h, skip_gain[h], skip)
        xbd[h] = jnp.where(chan == h, conv_f, 0.0).astype(BF)
    rest = base[...] + skip * conv_f
    for tb in range(2):
        rows = pl.ds(256 * tb, 256)
        cols = 256 * (tb + 1)
        inner = rest[256 * tb : 256 * tb + 256]
        for h in range(HEADS):
            inner = inner + jnp.dot(mix[h, rows, 0:cols], xbd[h, 0:cols, :], preferred_element_type=F32)
        out_ref[rows, :] = inner.astype(BF)
    weighted = (conv_f * weigh[...]).astype(BF)
    new_t = jnp.dot(inT[...], weighted, preferred_element_type=F32)
    fstate_ref[...] = carry[...] + new_t.T

    for copy in sends:
        copy.wait_send()


def put(*refs):
    srcs, dsts, sem = refs[0:3], refs[3:6], refs[6]
    copies = [pltpu.make_async_copy(src, dst, sem.at[k]) for k, (src, dst) in enumerate(zip(srcs, dsts))]
    for copy in copies:
        copy.start()
    for copy in copies:
        copy.wait()


def on_device(
    layer_input, proj_weight, step_weight, step_bias, decay_log, conv_weight, conv_bias, skip_gain,
    group_inputs, cached_state, cached_tail, owner_map, request_state, shared_id,
):
    smem = pl.BlockSpec(memory_space=pltpu.SMEM)
    vmem = pl.BlockSpec(memory_space=pltpu.VMEM)
    hbm = pl.BlockSpec(memory_space=pl.ANY)
    dma = pltpu.SemaphoreType.DMA
    shapes = (
        jax.ShapeDtypeStruct((TOK, CH), BF),
        jax.ShapeDtypeStruct((CH, N), F32),
        jax.ShapeDtypeStruct((3, 1, CH), F32),
    )
    args = (
        request_state, owner_map, shared_id, step_bias, decay_log, skip_gain,
        layer_input, proj_weight, step_weight.T, cached_tail.transpose(1, 0, 2), cached_state.reshape(CH, N), group_inputs.T,
        conv_weight, conv_bias.reshape(1, CH),
    )

    results = pl.pallas_call(
        body,
        out_shape=shapes,
        in_specs=[smem] * 6 + [hbm] * 6 + [vmem] * 2,
        out_specs=(vmem, vmem, vmem),
        scratch_shapes=[
            pltpu.VMEM((2, 2, 4, 4, 256, 256), BF),
            pltpu.VMEM((Z, 512, 256), BF),
            pltpu.VMEM((2 * HELD, 128, 256), BF),
            pltpu.VMEM((Z, 16, 256), BF),
            pltpu.VMEM((2, 4, 64, 512), BF),
            pltpu.VMEM((2, STEPS, 128, 256), BF),
            pltpu.VMEM((2, STEPS, 128, 256), BF),
            pltpu.VMEM((Z, 128), jnp.int32),
            pltpu.SMEM((Z, 128), jnp.int32),
            pltpu.VMEM((256, 256), F32),
            pltpu.VMEM((4, 512), BF),
            pltpu.VMEM((3, 1, 256), F32),
            pltpu.VMEM((512, 256), F32),
            pltpu.VMEM((2, 16, 512), F32),
            pltpu.VMEM((8 + TOK, 256), F32),
            pltpu.VMEM((256, 512), BF),
            pltpu.VMEM((512, 256), BF),
            pltpu.VMEM((512, 512), F32),
            pltpu.VMEM((4, 512, 512), BF),
            pltpu.VMEM((4, 512, 256), BF),
            pltpu.VMEM((2, 8, 512), F32),
            pltpu.VMEM((3, 512, 128), F32),
            pltpu.VMEM((512, 256), F32),
            pltpu.VMEM((512, 256), F32),
            pltpu.VMEM((256, 256), F32),
            dma((7,)),
            dma((2, 8, WSUB)),
            dma((2, 8, WSUB)),
            dma((2, 8, 1)),
            dma((2, 8, 1)),
            dma((2, 4, 4)),
            dma((2, 4, 4)),
            dma((2, 4)),
            dma((2, 4)),
            dma((5,)),
            dma((5,)),
            dma((2, STEPS)),
            dma((2, STEPS)),
            dma,
        ],
        compiler_params=pltpu.CompilerParams(
            collective_id=0, has_side_effects=True, vmem_limit_bytes=56 * 1024 * 1024
        ),
    )(*args)

    out, fstate, ftail = pl.pallas_call(
        put, out_shape=shapes, in_specs=[vmem] * 3, out_specs=[hbm] * 3, scratch_shapes=[dma((3,))]
    )(*results)
    return out, fstate.reshape(1, HEADS, 64, N), ftail.transpose(1, 0, 2)


def solution(mesh):
    return jax.shard_map(
        on_device,
        mesh=mesh,
        in_specs=(
            P("rep", "head"), P("rep", "head"), P("rep", "head"), P("head"), P("head"), P(None, "head"),
            P("head"), P("head"), P("rep", "head"), P("rep", "head", None, None), P("rep", None, "head"),
            P(), P(), P(),
        ),
        out_specs=(P("rep", "head"), P("rep", "head", None, None), P("rep", None, "head")),
        check_vma=False,
    )
```

```python
import jax
import jax.numpy as jnp
from jax import lax
from jax.experimental import pallas as pl
from jax.experimental.pallas import tpu as pltpu
from jax.sharding import PartitionSpec as P

MESH = pl.DeviceIdType.MESH
BF = jnp.bfloat16
F32 = jnp.float32
Z = 16
TOK = 512
CH = 256
HEADS = 4
N = 256
WSUB = 4
STEPS = 10
HELD = STEPS + 2
REACH = (10, 5)


def body(
    request_hbm, owner_hbm, shared_hbm, bias_hbm, decay_hbm, gain_hbm,
    x_hbm, w_hbm, sw_hbm, tail_hbm, state_hbm, g_hbm, cw_hbm, cb_hbm,
    out_hbm, fstate_hbm, ftail_hbm,
    out_ref, fstate_ref, ftail_ref,
    request_state, owner_map, shared_id, step_bias, decay_log, skip_gain, conv_w, conv_b,
    A, W, S, M, G, stage, landed, plan_v, plan, state_own, sw_own, tail_own, acc, sacc, ext, inT, outv, score, mix, xbd, rates, rate_t, base, weigh, carry,
    loc_sem, out_sem, ws_sem, wr_sem, ms_sem, mr_sem, as_sem, ar_sem, cs_sem, cr_sem, gs_sem, gr_sem, vs_sem, vr_sem, plan_sem,
):
    z = lax.axis_index("rep")
    hid = lax.axis_index("head")
    x, y, c = hid // 8, (hid // 2) % 4, hid % 2
    zr, zl = (z + 1) % Z, (z + Z - 1) % Z

    def dev(xx, yy, cc):
        return {"head": xx * 8 + yy * 2 + cc}

    xp, xm, yp, ym = (x + 1) % 4, (x + 3) % 4, (y + 1) % 4, (y + 3) % 4
    sibling = dev(x, y, 1 - c)
    zdev = ({"rep": zr}, {"rep": zl})
    pos = ((y, x), (x, y))
    x_nb, y_nb = (dev(xp, y, c), dev(xm, y, c)), (dev(x, yp, c), dev(x, ym, c))
    q_nb, p_nb = (x_nb, y_nb), (y_nb, x_nb)

    barrier = pltpu.get_barrier_semaphore()
    for d in (*zdev, *x_nb, *y_nb, sibling):
        pl.semaphore_signal(barrier, inc=1, device_id=d, device_id_type=MESH)

    sends = []

    def rcopy(src, dst, s_sem, r_sem, d):
        return pltpu.make_async_remote_copy(
            src_ref=src, dst_ref=dst, send_sem=s_sem, recv_sem=r_sem, device_id=d, device_id_type=MESH
        )

    def go(ref, s_sem, r_sem, d, dst=None):
        copy = rcopy(ref, ref if dst is None else dst, s_sem, r_sem, d)
        copy.start()
        sends.append(copy)

    def got(ref, s_sem, r_sem, d):
        rcopy(ref, ref, s_sem, r_sem, d).wait_recv()

    def slot(way, s):
        return s if way == 0 else (Z - s) % Z

    def ring(buf, rows, sub, s_sem, r_sem, way, s):
        here = buf.at[slot(way, s), rows]
        if s > 0:
            got(here, s_sem.at[way, s - 1, sub], r_sem.at[way, s - 1, sub], zdev[way])
        if s < 8 and not (s == 7 and sub not in last_subs(way, s_sem)):
            go(here, s_sem.at[way, s, sub], r_sem.at[way, s, sub], zdev[way], buf.at[slot(way, s + 1), rows])

    def last_subs(way, s_sem):
        if s_sem is ws_sem:
            return (0, 1) if way == 0 else (2, 3)
        return (0,) if way == 0 else ()

    def w_step(s, subs=range(WSUB)):
        for sub in subs:
            for way in (0, 1):
                if s < 8 or sub in last_subs(way, ws_sem):
                    ring(W, pl.ds(sub * (512 // WSUB), 512 // WSUB), sub, ws_sem, wr_sem, way, s)

    def early():
        pl.semaphore_wait(barrier, 7)
        for sub in (0, 1):
            rows = pl.ds(128 * sub, 128)
            for way in (0, 1):
                go(w_hbm.at[rows], ws_sem.at[way, 0, sub], wr_sem.at[way, 0, sub], zdev[way], W.at[slot(way, 1), rows])

    locs = [
        pltpu.make_async_copy(sw_hbm, sw_own, loc_sem.at[0]),
        pltpu.make_async_copy(tail_hbm, tail_own, loc_sem.at[1]),
        pltpu.make_async_copy(state_hbm, state_own, loc_sem.at[2]),
        pltpu.make_async_copy(w_hbm, W.at[0], loc_sem.at[3]),
        pltpu.make_async_copy(x_hbm.at[0:256], A.at[0, c, y, x], loc_sem.at[4]),
        pltpu.make_async_copy(x_hbm.at[256:512], A.at[1, c, x, y], loc_sem.at[5]),
        pltpu.make_async_copy(g_hbm, G.at[c, y], loc_sem.at[6]),
        pltpu.make_async_copy(request_hbm, request_state, loc_sem.at[7]),
        pltpu.make_async_copy(owner_hbm, owner_map, loc_sem.at[8]),
        pltpu.make_async_copy(shared_hbm, shared_id, loc_sem.at[9]),
        pltpu.make_async_copy(bias_hbm, step_bias, loc_sem.at[10]),
        pltpu.make_async_copy(decay_hbm, decay_log, loc_sem.at[11]),
        pltpu.make_async_copy(gain_hbm, skip_gain, loc_sem.at[12]),
        pltpu.make_async_copy(cw_hbm, conv_w, loc_sem.at[13]),
        pltpu.make_async_copy(cb_hbm, conv_b, loc_sem.at[14]),
    ]
    for copy in locs:
        copy.start()
    early()
    locs[0].wait()
    locs[1].wait()
    sw = sw_own[...].astype(F32)
    M[0] = jnp.concatenate(
        [sw[:, 0:256], sw[:, 256:512]] + [tail_own[k] for k in range(3)] + [jnp.zeros((5, CH), F32)], axis=0
    ).astype(BF)
    locs[2].wait()
    own = state_own[...].astype(BF)
    S[...] = jnp.zeros_like(S)
    for way in (0, 1):
        for part in (0, 1):
            S[way * HELD + part] = own[128 * part : 128 * part + 128]
    for i in range(3, 7):
        locs[i].wait()

    def state_row(q):
        sid = request_state[q]
        return owner_map[jnp.where(sid < Z, sid, shared_id[0])]

    def make_plan():
        pack = lax.broadcasted_iota(jnp.int32, (1, 64), 1)
        way, src, part = pack // 32, (pack % 32) // 2, pack % 2
        most = jnp.where(part == 0, REACH[0], REACH[1])
        togo = jnp.zeros((1, 64), jnp.int32)
        for q in range(Z):
            row = state_row(q)
            d = (q - row + Z) % Z
            ahead = jnp.where((d <= most) & (way == 0), d, 0)
            behind = jnp.where((d > most) & (way == 1), Z - d, 0)
            togo = jnp.maximum(togo, jnp.where(src == row, ahead + behind, 0))
        togo = togo.astype(F32)
        at = src
        name = (src * 2 + part + 1).astype(F32)
        code = (part + 1).astype(F32)
        order = pack.astype(F32)
        link_row = lax.broadcasted_iota(jnp.int32, (32, 64), 0)
        sent, came = [], []
        for t in range(STEPS):
            key = jnp.where(togo > 0.0, togo * 64.0 + order, 0.0)
            here = link_row == at + way * Z
            best = jnp.max(jnp.where(here, key, 0.0), axis=1, keepdims=True)
            wins = here & (key == best) & (key > 0.0)
            win = jnp.max(jnp.where(wins, 1.0, 0.0), axis=0, keepdims=True)
            then = jnp.where(way == 0, (at + 1) % Z, (at + Z - 1) % Z)
            sent.append(jnp.where(at == z, win * code, 0.0))
            came.append(jnp.where(then == z, win * name, 0.0))
            togo = togo - win
            code = jnp.where(win > 0.0, t + 3.0, code)
            at = jnp.where(win > 0.0, then, at)
        rest = [jnp.zeros((Z - STEPS, 64), F32)]
        sent, came = jnp.concatenate(sent + rest, axis=0), jnp.concatenate(came + rest, axis=0)
        half = lax.broadcasted_iota(jnp.int32, (Z, 64), 1) // 32
        lane = lax.broadcasted_iota(jnp.int32, (Z, 128), 1)
        table = jnp.zeros((Z, 128), F32)
        for k, (what, w) in enumerate(((sent, 0), (sent, 1), (came, 0), (came, 1))):
            column = jnp.max(jnp.where(half == w, what, 0.0), axis=1, keepdims=True)
            table = jnp.where(lane == k, column, table)
        plan_v[...] = table.astype(jnp.int32)
        copy = pltpu.make_async_copy(plan_v, plan, plan_sem)
        copy.start()
        copy.wait()

    def convey(t):
        for way in (0, 1):
            if t > 0:
                got(landed.at[way, t - 1], vs_sem.at[way, t - 1], vr_sem.at[way, t - 1], zdev[way])
                S[way * HELD + t + 1] = landed[way, t - 1]
            if t < STEPS:
                k = jnp.clip(plan[t, way] - 1, 0, HELD - 1)
                stage[way, t] = S[way * HELD + k]
                go(stage.at[way, t], vs_sem.at[way, t], vr_sem.at[way, t], zdev[way], landed.at[way, t])

    def prior_half(row, part):
        at = part
        for way in (0, 1):
            for t in range(STEPS):
                at = jnp.where(plan[t, 2 + way] == row * 2 + part + 1, way * HELD + t + 2, at)
        return S[at]

    def m_step(s):
        for way in (0, 1):
            if s < 8 or 0 in last_subs(way, ms_sem):
                ring(M, pl.ds(0, 16), 0, ms_sem, mr_sem, way, s)

    def ring4(stage, blk, halves, nb, s_sem, r_sem):
        if stage == 0:
            for way in (0, 1):
                go(blk(0), s_sem.at[way], r_sem.at[way], nb[way])
        elif stage == 1:
            for way, step in ((0, -1), (1, 1)):
                got(blk(step), s_sem.at[way], r_sem.at[way], nb[way])
                go(halves(blk(step), way), s_sem.at[2 + way], r_sem.at[2 + way], nb[way])
        else:
            for way in (0, 1):
                got(halves(blk(2), way), s_sem.at[2 + way], r_sem.at[2 + way], nb[way])

    def a_one(stage, i):
        p, q = pos[i]
        ring4(
            stage,
            lambda k: A.at[i, c, p, (q + 4 + k) % 4],
            lambda ref, way: ref.at[pl.ds(128 * way, 128)],
            q_nb[i], as_sem.at[i, 0], ar_sem.at[i, 0],
        )

    def a_two(stage, i):
        p, _ = pos[i]

        def part(k, piece):
            return A.at[i, c, (p + 4 + k) % 4, pl.ds(2 * piece, 2)]

        def sems(n, way):
            return as_sem.at[i, 1 + n, way], ar_sem.at[i, 1 + n, way]

        for way, step in ((0, -1), (1, 1)):
            d = p_nb[i][way]
            if stage == 0:
                go(part(0, way), *sems(0, way), d)
                go(part(0, 1 - way), *sems(1, way), d)
            elif stage == 1:
                got(part(step, way), *sems(0, way), d)
                go(part(step, way), *sems(2, way), d)
            elif stage == 2:
                got(part(step, 1 - way), *sems(1, way), d)
            else:
                got(part(2, way), *sems(2, way), d)

    def a_share(i, k):
        p, _ = pos[i]
        go(A.at[i, c, (p + k) % 4], cs_sem.at[i, k], cr_sem.at[i, k], sibling)

    def a_shared(i, k):
        p, _ = pos[i]
        got(A.at[i, 1 - c, (p + k) % 4], cs_sem.at[i, k], cr_sem.at[i, k], sibling)

    def g_ring(stage):
        ring4(
            stage,
            lambda k: G.at[c, (y + 4 + k) % 4],
            lambda ref, way: ref.at[pl.ds(32 * way, 32)],
            y_nb, gs_sem, gr_sem,
        )

    def a_block(i, kz, cc):
        ax, ay = kz // 4, kz % 4
        return A[0, cc, ay, ax] if i == 0 else A[1, cc, ax, ay]

    def project(j):
        kz = (z - j + Z) % Z
        for i in (0, 1):
            rows = pl.ds(256 * i, 256)
            part = jnp.dot(a_block(i, kz, 0), W[j, 0:256], preferred_element_type=F32)
            part += jnp.dot(a_block(i, kz, 1), W[j, 256:512], preferred_element_type=F32)
            acc[rows, :] += part

    def step_part(j):
        kz = (z - j + Z) % Z
        for i in (0, 1):
            for cc in (0, 1):
                sacc[cc, :, pl.ds(256 * i, 256)] += lax.dot_general(
                    M[j], a_block(i, kz, cc), (((1,), (1,)), ((), ())), preferred_element_type=F32
                )

    def vectors():
        for k in range(4):
            inT[pl.ds(64 * k, 64), :] = G[k % 2, k // 2]
            outv[:, pl.ds(64 * k, 64)] = G[k % 2, 2 + k // 2].astype(F32).T.astype(BF)

    def scores(tb):
        t0 = tb * 128
        cols = 256 if tb < 2 else 512
        sc = jnp.dot(outv[pl.ds(t0, 128), :], inT[:, 0:cols], preferred_element_type=F32)
        keep = lax.broadcasted_iota(jnp.int32, (128, cols), 1) <= t0 + lax.broadcasted_iota(jnp.int32, (128, cols), 0)
        score[pl.ds(t0, 128), 0:cols] = jnp.where(keep, sc, 0.0)

    def decays():
        row = lax.broadcasted_iota(jnp.int32, (8, 1), 0)

        def per_head(ref):
            col = jnp.zeros((8, 1), F32)
            for h in range(HEADS):
                col = jnp.where(row == h, ref[h], col)
            return col

        raw = jnp.concatenate([sacc[0, 0:4] + sacc[1, 4:8], jnp.zeros((4, TOK), F32)], axis=0)
        raw = raw + per_head(step_bias)
        step = jnp.maximum(raw, 0.0) + jnp.log1p(jnp.exp(-jnp.abs(raw)))
        decay = -jnp.exp(per_head(decay_log)) * step
        lane = lax.broadcasted_iota(jnp.int32, (8, TOK), 1)
        for k in range(9):
            decay = decay + jnp.where(lane >= 2**k, pltpu.roll(decay, 2**k, axis=1), 0.0)
        last = decay[:, TOK - 1 : TOK]
        weights = jnp.exp(last - decay) * step
        rates[0] = decay
        rates[1] = step
        decay_t = jnp.concatenate([decay, jnp.zeros((120, TOK), F32)], axis=0).T
        grown_t = jnp.exp(decay_t)
        weights_t = jnp.concatenate([weights, jnp.zeros((120, TOK), F32)], axis=0).T
        rate_t[0] = decay_t
        rate_t[1] = grown_t
        rate_t[2] = weights_t

    def make_mix(h):
        for tb in range(4):
            t0 = tb * 128
            cols = 256 if tb < 2 else 512
            differ = rate_t[0, t0 : t0 + 128, h : h + 1] - rates[0, h : h + 1, 0:cols]
            scaled = jnp.exp(jnp.minimum(differ, 0.0)) * rates[1, h : h + 1, 0:cols]
            mix[h, pl.ds(t0, 128), 0:cols] = (score[pl.ds(t0, 128), 0:cols] * scaled).astype(BF)

    def step_parts(first):
        @pl.loop(first, first + 4)
        def _(j):
            step_part(j)

    def projects(first, end):
        @pl.loop(first, end)
        def _(j):
            project(j)
            project(Z - j)

    def g_share():
        go(G.at[c], gs_sem.at[4], gr_sem.at[4], sibling)

    def g_shared():
        got(G.at[1 - c], gs_sem.at[4], gr_sem.at[4], sibling)

    def both(f, *args):
        for i in (0, 1):
            f(*args, i)

    def shared(i):
        for k in range(4):
            a_shared(i, k)

    chan = lax.broadcasted_iota(jnp.int32, (TOK, CH), 1) // 64

    def clear():
        acc[...] = jnp.zeros_like(acc)
        sacc[...] = jnp.zeros_like(sacc)

    def expand(cols):
        wide = jnp.broadcast_to(cols[:, 0:1], (TOK, CH))
        for h in range(1, HEADS):
            wide = jnp.where(chan == h, cols[:, h : h + 1], wide)
        return wide

    def expand_decays():
        base[...] = expand(rate_t[1])
        weigh[...] = expand(rate_t[2])

    def put_tail():
        j = (z - state_row(z) + Z) % Z
        ext[0:8, :] = jnp.concatenate([jnp.zeros((5, CH), F32), M[j].astype(F32)[8:11]], axis=0)

    def resume():
        row = state_row(z)
        prior = jnp.concatenate([prior_half(row, 0), prior_half(row, 1)], axis=0)
        base[...] *= lax.dot_general(outv[...], prior, (((1,), (1,)), ((), ())), preferred_element_type=F32)
        head_row = lax.broadcasted_iota(jnp.int32, (CH, 1), 0) // 64
        kept = jnp.zeros((CH, 1), F32)
        last_e = jnp.exp(rates[0, :, TOK - 1 : TOK])
        for h in range(HEADS):
            kept = jnp.where(head_row == h, last_e[h : h + 1, 0:1], kept)
        carry[...] = kept * prior.astype(F32)

    work = {u: [] for u in range(4 * 9)}

    def add(u, f, *args):
        work[u].append((f, args))

    for t in range(1, STEPS):
        add(2 + 33 * t // STEPS, convey, t)
    for s, u in enumerate((0, 4, 6, 8, 10, 13, 15, 18, 20)):
        if s:
            add(u, m_step, s)
    add(3, clear)
    add(5, both, a_one, 1)
    add(5, g_ring, 1)
    add(7, g_ring, 2)
    add(7, g_share)
    add(8, both, a_one, 2)
    add(8, both, a_two, 0)
    add(8, lambda: both(lambda i: a_share(i, 0)))
    add(11, g_shared)
    add(11, vectors)
    add(13, both, a_two, 1)
    for tb in range(4):
        add(12 + tb, scores, tb)
    add(16, both, a_two, 2)
    add(16, lambda: both(lambda i: (a_share(i, 3), a_share(i, 1))))
    add(19, both, a_two, 3)
    add(19, lambda: both(lambda i: a_share(i, 2)))
    add(21, both, shared)
    for k in range(4):
        add(21 + k, step_parts, 4 * k)
    add(24, decays)
    for h in range(HEADS):
        add(25 + h, make_mix, h)
    add(27, put_tail)
    add(28, expand_decays)
    add(28, project, 0)
    add(29, projects, 1, 3)
    add(30, projects, 3, 5)
    add(31, projects, 5, 7)
    add(32, projects, 7, 8)

    m_step(0)
    both(a_one, 0)
    for i in range(7, 15):
        locs[i].wait()
    make_plan()
    convey(0)
    w_step(0, (2, 3))
    g_ring(0)
    for u in range(3, 36):
        if u > 3:
            w_step(u // 4, (u % 4,))
        for f, args in work[u]:
            f(*args)

    leaving = []

    def leave(src, dst, k):
        copy = pltpu.make_async_copy(src, dst, out_sem.at[k])
        copy.start()
        leaving.append(copy)

    project(8)
    projected = acc[...].astype(BF).astype(F32)
    ext[8 : 8 + TOK, :] = projected
    for k in range(3):
        ftail_ref[k] = ext[TOK + 5 + k : TOK + 6 + k, :]
    leave(ftail_ref, ftail_hbm, 0)
    conv = conv_b[...] + conv_w[0:1, :] * ext[5 : 5 + TOK, :]
    for k in range(1, 4):
        conv = conv + conv_w[k : k + 1, :] * ext[5 + k : 5 + k + TOK, :]
    conv_f = (conv / (1.0 + jnp.exp(-conv))).astype(BF).astype(F32)
    skip = jnp.zeros((1, CH), F32)
    one = lax.broadcasted_iota(jnp.int32, (1, CH), 1) // 64
    for h in range(HEADS):
        skip = jnp.where(one == h, skip_gain[h], skip)
        xbd[h] = jnp.where(chan == h, conv_f, 0.0).astype(BF)
    for tb in range(2):
        rows = pl.ds(256 * tb, 256)
        cols = 256 * (tb + 1)
        inner = (skip * conv_f)[256 * tb : 256 * tb + 256]
        for h in range(HEADS):
            inner = inner + jnp.dot(mix[h, rows, 0:cols], xbd[h, 0:cols, :], preferred_element_type=F32)
        acc[rows, :] = inner
    weighted = (conv_f * weigh[...]).astype(BF)
    new_t = jnp.dot(inT[...], weighted, preferred_element_type=F32)
    convey(STEPS)
    resume()
    fstate_ref[...] = carry[...] + new_t.T
    leave(fstate_ref, fstate_hbm, 1)
    for tb in range(2):
        rows = pl.ds(256 * tb, 256)
        out_ref[rows, :] = (acc[rows, :] + base[rows, :]).astype(BF)
        leave(out_ref.at[rows], out_hbm.at[rows], 2 + tb)
    for copy in sends:
        copy.wait_send()
    for copy in leaving:
        copy.wait()


def put(*refs):
    srcs, dsts, sem = refs[0:3], refs[3:6], refs[6]
    copies = [pltpu.make_async_copy(src, dst, sem.at[k]) for k, (src, dst) in enumerate(zip(srcs, dsts))]
    for copy in copies:
        copy.start()
    for copy in copies:
        copy.wait()


def on_device(
    layer_input, proj_weight, step_weight, step_bias, decay_log, conv_weight, conv_bias, skip_gain,
    group_inputs, cached_state, cached_tail, owner_map, request_state, shared_id,
):
    smem = pl.BlockSpec(memory_space=pltpu.SMEM)
    vmem = pl.BlockSpec(memory_space=pltpu.VMEM)
    hbm = pl.BlockSpec(memory_space=pl.ANY)
    dma = pltpu.SemaphoreType.DMA
    shapes = (
        jax.ShapeDtypeStruct((TOK, CH), BF),
        jax.ShapeDtypeStruct((CH, N), F32),
        jax.ShapeDtypeStruct((3, 1, CH), F32),
    )
    args = (
        request_state, owner_map, shared_id, step_bias, decay_log, skip_gain,
        layer_input, proj_weight, step_weight.T, cached_tail.transpose(1, 0, 2), cached_state.reshape(CH, N), group_inputs.T,
        conv_weight, conv_bias.reshape(1, CH),
    )

    results = pl.pallas_call(
        body,
        out_shape=shapes,
        in_specs=[hbm] * 14,
        out_specs=(hbm, hbm, hbm),
        scratch_shapes=[
            *[pltpu.VMEM(v.shape, v.dtype) for v in shapes],
            pltpu.SMEM((16,), jnp.int32),
            pltpu.SMEM((16,), jnp.int32),
            pltpu.SMEM((1,), jnp.int32),
            pltpu.SMEM((4,), F32),
            pltpu.SMEM((4,), F32),
            pltpu.SMEM((4,), F32),
            pltpu.VMEM((4, 256), F32),
            pltpu.VMEM((1, 256), F32),
            pltpu.VMEM((2, 2, 4, 4, 256, 256), BF),
            pltpu.VMEM((Z, 512, 256), BF),
            pltpu.VMEM((2 * HELD, 128, 256), BF),
            pltpu.VMEM((Z, 16, 256), BF),
            pltpu.VMEM((2, 4, 64, 512), BF),
            pltpu.VMEM((2, STEPS, 128, 256), BF),
            pltpu.VMEM((2, STEPS, 128, 256), BF),
            pltpu.VMEM((Z, 128), jnp.int32),
            pltpu.SMEM((Z, 128), jnp.int32),
            pltpu.VMEM((256, 256), F32),
            pltpu.VMEM((4, 512), BF),
            pltpu.VMEM((3, 1, 256), F32),
            pltpu.VMEM((512, 256), F32),
            pltpu.VMEM((2, 16, 512), F32),
            pltpu.VMEM((8 + TOK, 256), F32),
            pltpu.VMEM((256, 512), BF),
            pltpu.VMEM((512, 256), BF),
            pltpu.VMEM((512, 512), F32),
            pltpu.VMEM((4, 512, 512), BF),
            pltpu.VMEM((4, 512, 256), BF),
            pltpu.VMEM((2, 8, 512), F32),
            pltpu.VMEM((3, 512, 128), F32),
            pltpu.VMEM((512, 256), F32),
            pltpu.VMEM((512, 256), F32),
            pltpu.VMEM((256, 256), F32),
            dma((15,)),
            dma((4,)),
            dma((2, 8, WSUB)),
            dma((2, 8, WSUB)),
            dma((2, 8, 1)),
            dma((2, 8, 1)),
            dma((2, 4, 4)),
            dma((2, 4, 4)),
            dma((2, 4)),
            dma((2, 4)),
            dma((5,)),
            dma((5,)),
            dma((2, STEPS)),
            dma((2, STEPS)),
            dma,
        ],
        compiler_params=pltpu.CompilerParams(
            collective_id=0, has_side_effects=True, vmem_limit_bytes=56 * 1024 * 1024
        ),
    )(*args)

    out, fstate, ftail = pl.pallas_call(
        put, out_shape=shapes, in_specs=[vmem] * 3, out_specs=[hbm] * 3, scratch_shapes=[dma((3,))]
    )(*results)
    return out, fstate.reshape(1, HEADS, 64, N), ftail.transpose(1, 0, 2)


def solution(mesh):
    return jax.shard_map(
        on_device,
        mesh=mesh,
        in_specs=(
            P("rep", "head"), P("rep", "head"), P("rep", "head"), P("head"), P("head"), P(None, "head"),
            P("head"), P("head"), P("rep", "head"), P("rep", "head", None, None), P("rep", None, "head"),
            P(), P(), P(),
        ),
        out_specs=(P("rep", "head"), P("rep", "head", None, None), P("rep", None, "head")),
        check_vma=False,
    )
```

```python
import jax
import jax.numpy as jnp
from jax import lax
from jax.experimental import pallas as pl
from jax.experimental.pallas import tpu as pltpu
from jax.sharding import PartitionSpec as P

MESH = pl.DeviceIdType.MESH
BF = jnp.bfloat16
F32 = jnp.float32
Z = 16
TOK = 512
CH = 256
HEADS = 4
N = 256
WSUB = 4
STEPS = 10
HELD = STEPS + 2
REACH = (10, 5)


def body(
    request_hbm, owner_hbm, shared_hbm, bias_hbm, decay_hbm, gain_hbm,
    x_hbm, w_hbm, sw_hbm, tail_hbm, state_hbm, g_hbm, cw_hbm, cb_hbm,
    out_hbm, fstate_hbm, ftail_hbm,
    out_ref, fstate_ref, ftail_ref,
    request_state, owner_map, shared_id, step_bias, decay_log, skip_gain, conv_w, conv_b,
    A, W, S, M, G, stage, landed, plan_v, plan, state_own, sw_own, tail_own, acc, sacc, ext, inT, outv, score, mix, xbd, rates, rate_t, base, weigh, carry,
    loc_sem, out_sem, ws_sem, wr_sem, ms_sem, mr_sem, as_sem, ar_sem, cs_sem, cr_sem, gs_sem, gr_sem, vs_sem, vr_sem, plan_sem,
):
    z = lax.axis_index("rep")
    hid = lax.axis_index("head")
    x, y, c = hid // 8, (hid // 2) % 4, hid % 2
    zr, zl = (z + 1) % Z, (z + Z - 1) % Z

    def dev(xx, yy, cc):
        return {"head": xx * 8 + yy * 2 + cc}

    xp, xm, yp, ym = (x + 1) % 4, (x + 3) % 4, (y + 1) % 4, (y + 3) % 4
    sibling = dev(x, y, 1 - c)
    zdev = ({"rep": zr}, {"rep": zl})
    pos = ((y, x), (x, y))
    x_nb, y_nb = (dev(xp, y, c), dev(xm, y, c)), (dev(x, yp, c), dev(x, ym, c))
    q_nb, p_nb = (x_nb, y_nb), (y_nb, x_nb)

    barrier = pltpu.get_barrier_semaphore()
    for d in (*zdev, *x_nb, *y_nb, sibling):
        pl.semaphore_signal(barrier, inc=1, device_id=d, device_id_type=MESH)

    sends = []

    def rcopy(src, dst, s_sem, r_sem, d):
        return pltpu.make_async_remote_copy(
            src_ref=src, dst_ref=dst, send_sem=s_sem, recv_sem=r_sem, device_id=d, device_id_type=MESH
        )

    def go(ref, s_sem, r_sem, d, dst=None):
        copy = rcopy(ref, ref if dst is None else dst, s_sem, r_sem, d)
        copy.start()
        sends.append(copy)

    def got(ref, s_sem, r_sem, d):
        rcopy(ref, ref, s_sem, r_sem, d).wait_recv()

    def slot(way, s):
        return s if way == 0 else (Z - s) % Z

    def ring(buf, rows, sub, s_sem, r_sem, way, s):
        here = buf.at[slot(way, s), rows]
        if s > 0:
            got(here, s_sem.at[way, s - 1, sub], r_sem.at[way, s - 1, sub], zdev[way])
        if s < 8 and not (s == 7 and sub not in last_subs(way, s_sem)):
            go(here, s_sem.at[way, s, sub], r_sem.at[way, s, sub], zdev[way], buf.at[slot(way, s + 1), rows])

    def last_subs(way, s_sem):
        if s_sem is ws_sem:
            return (0, 1) if way == 0 else (2, 3)
        return (0,) if way == 0 else ()

    def w_step(s, subs=range(WSUB)):
        for sub in subs:
            for way in (0, 1):
                if s < 8 or sub in last_subs(way, ws_sem):
                    ring(W, pl.ds(sub * (512 // WSUB), 512 // WSUB), sub, ws_sem, wr_sem, way, s)

    def early():
        pl.semaphore_wait(barrier, 7)
        for sub in (0, 1):
            rows = pl.ds(128 * sub, 128)
            for way in (0, 1):
                go(w_hbm.at[rows], ws_sem.at[way, 0, sub], wr_sem.at[way, 0, sub], zdev[way], W.at[slot(way, 1), rows])

    locs = [
        pltpu.make_async_copy(sw_hbm, sw_own, loc_sem.at[0]),
        pltpu.make_async_copy(tail_hbm, tail_own, loc_sem.at[1]),
        pltpu.make_async_copy(state_hbm, state_own, loc_sem.at[2]),
        pltpu.make_async_copy(w_hbm, W.at[0], loc_sem.at[3]),
        pltpu.make_async_copy(x_hbm.at[0:256], A.at[0, c, y, x], loc_sem.at[4]),
        pltpu.make_async_copy(x_hbm.at[256:512], A.at[1, c, x, y], loc_sem.at[5]),
        pltpu.make_async_copy(g_hbm, G.at[c, y], loc_sem.at[6]),
        pltpu.make_async_copy(request_hbm, request_state, loc_sem.at[7]),
        pltpu.make_async_copy(owner_hbm, owner_map, loc_sem.at[8]),
        pltpu.make_async_copy(shared_hbm, shared_id, loc_sem.at[9]),
        pltpu.make_async_copy(bias_hbm, step_bias, loc_sem.at[10]),
        pltpu.make_async_copy(decay_hbm, decay_log, loc_sem.at[11]),
        pltpu.make_async_copy(gain_hbm, skip_gain, loc_sem.at[12]),
        pltpu.make_async_copy(cw_hbm, conv_w, loc_sem.at[13]),
        pltpu.make_async_copy(cb_hbm, conv_b, loc_sem.at[14]),
    ]
    for copy in locs:
        copy.start()
    early()
    locs[0].wait()
    locs[1].wait()
    sw = sw_own[...].astype(F32)
    M[0] = jnp.concatenate(
        [sw[:, 0:256], sw[:, 256:512]] + [tail_own[k] for k in range(3)] + [jnp.zeros((5, CH), F32)], axis=0
    ).astype(BF)
    locs[2].wait()
    own = state_own[...].astype(BF)
    S[...] = jnp.zeros_like(S)
    for way in (0, 1):
        for part in (0, 1):
            S[way * HELD + part] = own[128 * part : 128 * part + 128]
    for i in range(3, 7):
        locs[i].wait()

    def state_row(q):
        sid = request_state[q]
        return owner_map[jnp.where(sid < Z, sid, shared_id[0])]

    def make_plan():
        pack = lax.broadcasted_iota(jnp.int32, (1, 64), 1)
        way, src, part = pack // 32, (pack % 32) // 2, pack % 2
        most = jnp.where(part == 0, REACH[0], REACH[1])
        togo = jnp.zeros((1, 64), jnp.int32)
        for q in range(Z):
            row = state_row(q)
            d = (q - row + Z) % Z
            ahead = jnp.where((d <= most) & (way == 0), d, 0)
            behind = jnp.where((d > most) & (way == 1), Z - d, 0)
            togo = jnp.maximum(togo, jnp.where(src == row, ahead + behind, 0))
        togo = togo.astype(F32)
        at = src
        name = (src * 2 + part + 1).astype(F32)
        code = (part + 1).astype(F32)
        order = pack.astype(F32)
        link_row = lax.broadcasted_iota(jnp.int32, (32, 64), 0)
        sent, came = [], []
        for t in range(STEPS):
            key = jnp.where(togo > 0.0, togo * 64.0 + order, 0.0)
            here = link_row == at + way * Z
            best = jnp.max(jnp.where(here, key, 0.0), axis=1, keepdims=True)
            wins = here & (key == best) & (key > 0.0)
            win = jnp.max(jnp.where(wins, 1.0, 0.0), axis=0, keepdims=True)
            then = jnp.where(way == 0, (at + 1) % Z, (at + Z - 1) % Z)
            sent.append(jnp.where(at == z, win * code, 0.0))
            came.append(jnp.where(then == z, win * name, 0.0))
            togo = togo - win
            code = jnp.where(win > 0.0, t + 3.0, code)
            at = jnp.where(win > 0.0, then, at)
        rest = [jnp.zeros((Z - STEPS, 64), F32)]
        sent, came = jnp.concatenate(sent + rest, axis=0), jnp.concatenate(came + rest, axis=0)
        half = lax.broadcasted_iota(jnp.int32, (Z, 64), 1) // 32
        lane = lax.broadcasted_iota(jnp.int32, (Z, 128), 1)
        table = jnp.zeros((Z, 128), F32)
        for k, (what, w) in enumerate(((sent, 0), (sent, 1), (came, 0), (came, 1))):
            column = jnp.max(jnp.where(half == w, what, 0.0), axis=1, keepdims=True)
            table = jnp.where(lane == k, column, table)
        plan_v[...] = table.astype(jnp.int32)
        copy = pltpu.make_async_copy(plan_v, plan, plan_sem)
        copy.start()
        copy.wait()

    def convey(t):
        for way in (0, 1):
            if t > 0:
                got(landed.at[way, t - 1], vs_sem.at[way, t - 1], vr_sem.at[way, t - 1], zdev[way])
                S[way * HELD + t + 1] = landed[way, t - 1]
            if t < STEPS:
                k = jnp.clip(plan[t, way] - 1, 0, HELD - 1)
                stage[way, t] = S[way * HELD + k]
                go(stage.at[way, t], vs_sem.at[way, t], vr_sem.at[way, t], zdev[way], landed.at[way, t])

    def prior_half(row, part):
        at = part
        for way in (0, 1):
            for t in range(STEPS):
                at = jnp.where(plan[t, 2 + way] == row * 2 + part + 1, way * HELD + t + 2, at)
        return S[at]

    def m_step(s):
        for way in (0, 1):
            if s < 8 or 0 in last_subs(way, ms_sem):
                ring(M, pl.ds(0, 16), 0, ms_sem, mr_sem, way, s)

    def ring4(stage, blk, halves, nb, s_sem, r_sem):
        if stage == 0:
            for way in (0, 1):
                go(blk(0), s_sem.at[way], r_sem.at[way], nb[way])
        elif stage == 1:
            for way, step in ((0, -1), (1, 1)):
                got(blk(step), s_sem.at[way], r_sem.at[way], nb[way])
                go(halves(blk(step), way), s_sem.at[2 + way], r_sem.at[2 + way], nb[way])
        else:
            for way in (0, 1):
                got(halves(blk(2), way), s_sem.at[2 + way], r_sem.at[2 + way], nb[way])

    def a_one(stage, i):
        p, q = pos[i]
        ring4(
            stage,
            lambda k: A.at[i, c, p, (q + 4 + k) % 4],
            lambda ref, way: ref.at[pl.ds(128 * way, 128)],
            q_nb[i], as_sem.at[i, 0], ar_sem.at[i, 0],
        )

    def a_two(stage, i):
        p, _ = pos[i]

        def part(k, piece):
            return A.at[i, c, (p + 4 + k) % 4, pl.ds(2 * piece, 2)]

        def sems(n, way):
            return as_sem.at[i, 1 + n, way], ar_sem.at[i, 1 + n, way]

        for way, step in ((0, -1), (1, 1)):
            d = p_nb[i][way]
            if stage == 0:
                go(part(0, way), *sems(0, way), d)
                go(part(0, 1 - way), *sems(1, way), d)
            elif stage == 1:
                got(part(step, way), *sems(0, way), d)
                go(part(step, way), *sems(2, way), d)
            elif stage == 2:
                got(part(step, 1 - way), *sems(1, way), d)
            else:
                got(part(2, way), *sems(2, way), d)

    def a_share(i, k):
        p, _ = pos[i]
        go(A.at[i, c, (p + k) % 4], cs_sem.at[i, k], cr_sem.at[i, k], sibling)

    def a_shared(i, k):
        p, _ = pos[i]
        got(A.at[i, 1 - c, (p + k) % 4], cs_sem.at[i, k], cr_sem.at[i, k], sibling)

    def g_ring(stage):
        ring4(
            stage,
            lambda k: G.at[c, (y + 4 + k) % 4],
            lambda ref, way: ref.at[pl.ds(32 * way, 32)],
            y_nb, gs_sem, gr_sem,
        )

    def a_block(i, kz, cc):
        ax, ay = kz // 4, kz % 4
        return A[0, cc, ay, ax] if i == 0 else A[1, cc, ax, ay]

    def project(j):
        kz = (z - j + Z) % Z
        for i in (0, 1):
            rows = pl.ds(256 * i, 256)
            part = jnp.dot(a_block(i, kz, 0), W[j, 0:256], preferred_element_type=F32)
            part += jnp.dot(a_block(i, kz, 1), W[j, 256:512], preferred_element_type=F32)
            acc[rows, :] += part

    def step_part(j):
        kz = (z - j + Z) % Z
        for i in (0, 1):
            for cc in (0, 1):
                sacc[cc, :, pl.ds(256 * i, 256)] += lax.dot_general(
                    M[j], a_block(i, kz, cc), (((1,), (1,)), ((), ())), preferred_element_type=F32
                )

    def vectors():
        for k in range(4):
            inT[pl.ds(64 * k, 64), :] = G[k % 2, k // 2]
            outv[:, pl.ds(64 * k, 64)] = G[k % 2, 2 + k // 2].astype(F32).T.astype(BF)

    def scores(tb):
        t0 = tb * 128
        cols = 256 if tb < 2 else 512
        sc = jnp.dot(outv[pl.ds(t0, 128), :], inT[:, 0:cols], preferred_element_type=F32)
        keep = lax.broadcasted_iota(jnp.int32, (128, cols), 1) <= t0 + lax.broadcasted_iota(jnp.int32, (128, cols), 0)
        score[pl.ds(t0, 128), 0:cols] = jnp.where(keep, sc, 0.0)

    def decays():
        row = lax.broadcasted_iota(jnp.int32, (8, 1), 0)

        def per_head(ref):
            col = jnp.zeros((8, 1), F32)
            for h in range(HEADS):
                col = jnp.where(row == h, ref[h], col)
            return col

        raw = jnp.concatenate([sacc[0, 0:4] + sacc[1, 4:8], jnp.zeros((4, TOK), F32)], axis=0)
        raw = raw + per_head(step_bias)
        step = jnp.maximum(raw, 0.0) + jnp.log1p(jnp.exp(-jnp.abs(raw)))
        decay = -jnp.exp(per_head(decay_log)) * step
        lane = lax.broadcasted_iota(jnp.int32, (8, TOK), 1)
        for k in range(9):
            decay = decay + jnp.where(lane >= 2**k, pltpu.roll(decay, 2**k, axis=1), 0.0)
        last = decay[:, TOK - 1 : TOK]
        weights = jnp.exp(last - decay) * step
        rates[0] = decay
        rates[1] = step
        decay_t = jnp.concatenate([decay, jnp.zeros((120, TOK), F32)], axis=0).T
        grown_t = jnp.exp(decay_t)
        weights_t = jnp.concatenate([weights, jnp.zeros((120, TOK), F32)], axis=0).T
        rate_t[0] = decay_t
        rate_t[1] = grown_t
        rate_t[2] = weights_t

    def make_mix(h):
        for tb in range(4):
            t0 = tb * 128
            cols = 256 if tb < 2 else 512
            differ = rate_t[0, t0 : t0 + 128, h : h + 1] - rates[0, h : h + 1, 0:cols]
            scaled = jnp.exp(jnp.minimum(differ, 0.0)) * rates[1, h : h + 1, 0:cols]
            mix[h, pl.ds(t0, 128), 0:cols] = (score[pl.ds(t0, 128), 0:cols] * scaled).astype(BF)

    def step_parts(first):
        @pl.loop(first, first + 4)
        def _(j):
            step_part(j)

    def projects(first, end):
        @pl.loop(first, end)
        def _(j):
            project(j)
            project(Z - j)

    def g_share():
        go(G.at[c], gs_sem.at[4], gr_sem.at[4], sibling)

    def g_shared():
        got(G.at[1 - c], gs_sem.at[4], gr_sem.at[4], sibling)

    def both(f, *args):
        for i in (0, 1):
            f(*args, i)

    def shared(i):
        for k in range(4):
            a_shared(i, k)

    chan = lax.broadcasted_iota(jnp.int32, (TOK, CH), 1) // 64

    def clear():
        acc[...] = jnp.zeros_like(acc)
        sacc[...] = jnp.zeros_like(sacc)

    def expand(cols):
        wide = jnp.broadcast_to(cols[:, 0:1], (TOK, CH))
        for h in range(1, HEADS):
            wide = jnp.where(chan == h, cols[:, h : h + 1], wide)
        return wide

    def expand_decays():
        base[...] = expand(rate_t[1])
        weigh[...] = expand(rate_t[2])

    def put_tail():
        j = (z - state_row(z) + Z) % Z
        ext[0:8, :] = jnp.concatenate([jnp.zeros((5, CH), F32), M[j].astype(F32)[8:11]], axis=0)

    def resume():
        row = state_row(z)
        prior = jnp.concatenate([prior_half(row, 0), prior_half(row, 1)], axis=0)
        base[...] *= lax.dot_general(outv[...], prior, (((1,), (1,)), ((), ())), preferred_element_type=F32)
        head_row = lax.broadcasted_iota(jnp.int32, (CH, 1), 0) // 64
        kept = jnp.zeros((CH, 1), F32)
        last_e = jnp.exp(rates[0, :, TOK - 1 : TOK])
        for h in range(HEADS):
            kept = jnp.where(head_row == h, last_e[h : h + 1, 0:1], kept)
        carry[...] = kept * prior.astype(F32)

    work = {u: [] for u in range(4 * 9)}

    def add(u, f, *args):
        work[u].append((f, args))

    for t in range(1, STEPS):
        add(2 + 33 * t // STEPS, convey, t)
    for s, u in enumerate((0, 4, 6, 8, 10, 13, 15, 18, 20)):
        if s:
            add(u, m_step, s)
    add(3, clear)
    add(5, both, a_one, 1)
    add(5, g_ring, 1)
    add(7, g_ring, 2)
    add(7, g_share)
    add(8, both, a_one, 2)
    add(8, both, a_two, 0)
    add(8, lambda: both(lambda i: a_share(i, 0)))
    add(11, g_shared)
    add(11, vectors)
    add(13, both, a_two, 1)
    for tb in range(4):
        add(12 + tb, scores, tb)
    add(16, both, a_two, 2)
    add(16, lambda: both(lambda i: (a_share(i, 3), a_share(i, 1))))
    add(19, both, a_two, 3)
    add(19, lambda: both(lambda i: a_share(i, 2)))
    add(21, both, shared)
    for k in range(4):
        add(21 + k, step_parts, 4 * k)
    add(24, decays)
    for h in range(HEADS):
        add(25 + h, make_mix, h)
    add(27, put_tail)
    add(28, expand_decays)
    add(28, project, 0)
    add(29, projects, 1, 3)
    add(30, projects, 3, 5)
    add(31, projects, 5, 7)
    add(32, projects, 7, 8)

    m_step(0)
    both(a_one, 0)
    for i in range(7, 15):
        locs[i].wait()
    make_plan()
    convey(0)
    w_step(0, (2, 3))
    g_ring(0)
    for u in range(3, 36):
        if u > 3:
            w_step(u // 4, (u % 4,))
        for f, args in work[u]:
            f(*args)

    leaving = []

    def leave(src, dst, k):
        copy = pltpu.make_async_copy(src, dst, out_sem.at[k])
        copy.start()
        leaving.append(copy)

    project(8)
    projected = acc[...].astype(BF).astype(F32)
    ext[8 : 8 + TOK, :] = projected
    for k in range(3):
        ftail_ref[k] = ext[TOK + 5 + k : TOK + 6 + k, :]
    leave(ftail_ref, ftail_hbm, 0)
    conv = conv_b[...] + conv_w[0:1, :] * ext[5 : 5 + TOK, :]
    for k in range(1, 4):
        conv = conv + conv_w[k : k + 1, :] * ext[5 + k : 5 + k + TOK, :]
    conv_f = (conv / (1.0 + jnp.exp(-conv))).astype(BF).astype(F32)
    skip = jnp.zeros((1, CH), F32)
    one = lax.broadcasted_iota(jnp.int32, (1, CH), 1) // 64
    for h in range(HEADS):
        skip = jnp.where(one == h, skip_gain[h], skip)
        xbd[h] = jnp.where(chan == h, conv_f, 0.0).astype(BF)
    for tb in range(2):
        rows = pl.ds(256 * tb, 256)
        cols = 256 * (tb + 1)
        inner = (skip * conv_f)[256 * tb : 256 * tb + 256]
        for h in range(HEADS):
            inner = inner + jnp.dot(mix[h, rows, 0:cols], xbd[h, 0:cols, :], preferred_element_type=F32)
        acc[rows, :] = inner
    weighted = (conv_f * weigh[...]).astype(BF)
    new_t = jnp.dot(inT[...], weighted, preferred_element_type=F32)
    convey(STEPS)
    resume()
    fstate_ref[...] = carry[...] + new_t.T
    leave(fstate_ref, fstate_hbm, 1)
    for tb in range(2):
        rows = pl.ds(256 * tb, 256)
        out_ref[rows, :] = (acc[rows, :] + base[rows, :]).astype(BF)
        leave(out_ref.at[rows], out_hbm.at[rows], 2 + tb)
    for copy in sends:
        copy.wait_send()
    for copy in leaving:
        copy.wait()


def put(*refs):
    srcs, dsts, sem = refs[0:3], refs[3:6], refs[6]
    copies = [pltpu.make_async_copy(src, dst, sem.at[k]) for k, (src, dst) in enumerate(zip(srcs, dsts))]
    for copy in copies:
        copy.start()
    for copy in copies:
        copy.wait()


def on_device(
    layer_input, proj_weight, step_weight, step_bias, decay_log, conv_weight, conv_bias, skip_gain,
    group_inputs, cached_state, cached_tail, owner_map, request_state, shared_id,
):
    smem = pl.BlockSpec(memory_space=pltpu.SMEM)
    vmem = pl.BlockSpec(memory_space=pltpu.VMEM)
    hbm = pl.BlockSpec(memory_space=pl.ANY)
    dma = pltpu.SemaphoreType.DMA
    shapes = (
        jax.ShapeDtypeStruct((TOK, CH), BF),
        jax.ShapeDtypeStruct((CH, N), F32),
        jax.ShapeDtypeStruct((3, 1, CH), F32),
    )
    args = (
        request_state, owner_map, shared_id, step_bias, decay_log, skip_gain,
        layer_input, proj_weight, step_weight.T, cached_tail.transpose(1, 0, 2), cached_state.reshape(CH, N), group_inputs.T,
        conv_weight, conv_bias.reshape(1, CH),
    )

    results = pl.pallas_call(
        body,
        out_shape=shapes,
        in_specs=[hbm] * 14,
        out_specs=(hbm, hbm, hbm),
        scratch_shapes=[
            *[pltpu.VMEM(v.shape, v.dtype) for v in shapes],
            pltpu.SMEM((16,), jnp.int32),
            pltpu.SMEM((16,), jnp.int32),
            pltpu.SMEM((1,), jnp.int32),
            pltpu.SMEM((4,), F32),
            pltpu.SMEM((4,), F32),
            pltpu.SMEM((4,), F32),
            pltpu.VMEM((4, 256), F32),
            pltpu.VMEM((1, 256), F32),
            pltpu.VMEM((2, 2, 4, 4, 256, 256), BF),
            pltpu.VMEM((Z, 512, 256), BF),
            pltpu.VMEM((2 * HELD, 128, 256), BF),
            pltpu.VMEM((Z, 16, 256), BF),
            pltpu.VMEM((2, 4, 64, 512), BF),
            pltpu.VMEM((2, STEPS, 128, 256), BF),
            pltpu.VMEM((2, STEPS, 128, 256), BF),
            pltpu.VMEM((Z, 128), jnp.int32),
            pltpu.SMEM((Z, 128), jnp.int32),
            pltpu.VMEM((256, 256), F32),
            pltpu.VMEM((4, 512), BF),
            pltpu.VMEM((3, 1, 256), F32),
            pltpu.VMEM((512, 256), F32),
            pltpu.VMEM((2, 16, 512), F32),
            pltpu.VMEM((8 + TOK, 256), F32),
            pltpu.VMEM((256, 512), BF),
            pltpu.VMEM((512, 256), BF),
            pltpu.VMEM((512, 512), F32),
            pltpu.VMEM((4, 512, 512), BF),
            pltpu.VMEM((4, 512, 256), BF),
            pltpu.VMEM((2, 8, 512), F32),
            pltpu.VMEM((3, 512, 128), F32),
            pltpu.VMEM((512, 256), F32),
            pltpu.VMEM((512, 256), F32),
            pltpu.VMEM((256, 256), F32),
            dma((15,)),
            dma((4,)),
            dma((2, 8, WSUB)),
            dma((2, 8, WSUB)),
            dma((2, 8, 1)),
            dma((2, 8, 1)),
            dma((2, 4, 4)),
            dma((2, 4, 4)),
            dma((2, 4)),
            dma((2, 4)),
            dma((5,)),
            dma((5,)),
            dma((2, STEPS)),
            dma((2, STEPS)),
            dma,
        ],
        compiler_params=pltpu.CompilerParams(
            collective_id=0, has_side_effects=True, vmem_limit_bytes=56 * 1024 * 1024
        ),
    )(*args)

    results = lax.cond(shared_id[0] >= 0, lambda *v: v, lambda *v: tuple(jnp.zeros_like(u) for u in v), *results)
    out, fstate, ftail = pl.pallas_call(
        put, out_shape=shapes, in_specs=[vmem] * 3, out_specs=[hbm] * 3, scratch_shapes=[dma((3,))]
    )(*results)
    return out, fstate.reshape(1, HEADS, 64, N), ftail.transpose(1, 0, 2)


def solution(mesh):
    return jax.shard_map(
        on_device,
        mesh=mesh,
        in_specs=(
            P("rep", "head"), P("rep", "head"), P("rep", "head"), P("head"), P("head"), P(None, "head"),
            P("head"), P("head"), P("rep", "head"), P("rep", "head", None, None), P("rep", None, "head"),
            P(), P(), P(),
        ),
        out_specs=(P("rep", "head"), P("rep", "head", None, None), P("rep", None, "head")),
        check_vma=False,
    )
```

```python
import jax
import jax.numpy as jnp
from jax import lax
from jax.experimental import pallas as pl
from jax.experimental.pallas import tpu as pltpu
from jax.sharding import PartitionSpec as P

MESH = pl.DeviceIdType.MESH
BF = jnp.bfloat16
F32 = jnp.float32
Z = 16
TOK = 512
CH = 256
HEADS = 4
N = 256
WSUB = 4
STEPS = 10
HELD = STEPS + 2
REACH = (10, 5)


def body(
    request_hbm, owner_hbm, shared_hbm, bias_hbm, decay_hbm, gain_hbm,
    x_hbm, w_hbm, sw_hbm, tail_hbm, state_hbm, g_hbm, cw_hbm, cb_hbm,
    out_ref, fstate_ref, ftail_ref,
    request_state, owner_map, shared_id, step_bias, decay_log, skip_gain, conv_w, conv_b,
    A, W, S, M, G, stage, landed, plan_v, plan, state_own, sw_own, tail_own, acc, sacc, ext, inT, outv, score, mix, xbd, rates, rate_t, base, weigh, carry,
    loc_sem, ws_sem, wr_sem, ms_sem, mr_sem, as_sem, ar_sem, cs_sem, cr_sem, gs_sem, gr_sem, vs_sem, vr_sem, plan_sem,
):
    z = lax.axis_index("rep")
    hid = lax.axis_index("head")
    x, y, c = hid // 8, (hid // 2) % 4, hid % 2
    zr, zl = (z + 1) % Z, (z + Z - 1) % Z

    def dev(xx, yy, cc):
        return {"head": xx * 8 + yy * 2 + cc}

    xp, xm, yp, ym = (x + 1) % 4, (x + 3) % 4, (y + 1) % 4, (y + 3) % 4
    sibling = dev(x, y, 1 - c)
    zdev = ({"rep": zr}, {"rep": zl})
    pos = ((y, x), (x, y))
    x_nb, y_nb = (dev(xp, y, c), dev(xm, y, c)), (dev(x, yp, c), dev(x, ym, c))
    q_nb, p_nb = (x_nb, y_nb), (y_nb, x_nb)

    barrier = pltpu.get_barrier_semaphore()
    for d in (*zdev, *x_nb, *y_nb, sibling):
        pl.semaphore_signal(barrier, inc=1, device_id=d, device_id_type=MESH)

    sends = []

    def rcopy(src, dst, s_sem, r_sem, d):
        return pltpu.make_async_remote_copy(
            src_ref=src, dst_ref=dst, send_sem=s_sem, recv_sem=r_sem, device_id=d, device_id_type=MESH
        )

    def go(ref, s_sem, r_sem, d, dst=None):
        copy = rcopy(ref, ref if dst is None else dst, s_sem, r_sem, d)
        copy.start()
        sends.append(copy)

    def got(ref, s_sem, r_sem, d):
        rcopy(ref, ref, s_sem, r_sem, d).wait_recv()

    def slot(way, s):
        return s if way == 0 else (Z - s) % Z

    def ring(buf, rows, sub, s_sem, r_sem, way, s):
        here = buf.at[slot(way, s), rows]
        if s > 0:
            got(here, s_sem.at[way, s - 1, sub], r_sem.at[way, s - 1, sub], zdev[way])
        if s < 8 and not (s == 7 and sub not in last_subs(way, s_sem)):
            go(here, s_sem.at[way, s, sub], r_sem.at[way, s, sub], zdev[way], buf.at[slot(way, s + 1), rows])

    def last_subs(way, s_sem):
        if s_sem is ws_sem:
            return (0, 1) if way == 0 else (2, 3)
        return (0,) if way == 0 else ()

    def w_step(s, subs=range(WSUB)):
        for sub in subs:
            for way in (0, 1):
                if s < 8 or sub in last_subs(way, ws_sem):
                    ring(W, pl.ds(sub * (512 // WSUB), 512 // WSUB), sub, ws_sem, wr_sem, way, s)

    def early():
        pl.semaphore_wait(barrier, 7)
        for sub in (0, 1):
            rows = pl.ds(128 * sub, 128)
            for way in (0, 1):
                go(w_hbm.at[rows], ws_sem.at[way, 0, sub], wr_sem.at[way, 0, sub], zdev[way], W.at[slot(way, 1), rows])

    locs = [
        pltpu.make_async_copy(sw_hbm, sw_own, loc_sem.at[0]),
        pltpu.make_async_copy(tail_hbm, tail_own, loc_sem.at[1]),
        pltpu.make_async_copy(state_hbm, state_own, loc_sem.at[2]),
        pltpu.make_async_copy(w_hbm, W.at[0], loc_sem.at[3]),
        pltpu.make_async_copy(x_hbm.at[0:256], A.at[0, c, y, x], loc_sem.at[4]),
        pltpu.make_async_copy(x_hbm.at[256:512], A.at[1, c, x, y], loc_sem.at[5]),
        pltpu.make_async_copy(g_hbm, G.at[c, y], loc_sem.at[6]),
        pltpu.make_async_copy(request_hbm, request_state, loc_sem.at[7]),
        pltpu.make_async_copy(owner_hbm, owner_map, loc_sem.at[8]),
        pltpu.make_async_copy(shared_hbm, shared_id, loc_sem.at[9]),
        pltpu.make_async_copy(bias_hbm, step_bias, loc_sem.at[10]),
        pltpu.make_async_copy(decay_hbm, decay_log, loc_sem.at[11]),
        pltpu.make_async_copy(gain_hbm, skip_gain, loc_sem.at[12]),
        pltpu.make_async_copy(cw_hbm, conv_w, loc_sem.at[13]),
        pltpu.make_async_copy(cb_hbm, conv_b, loc_sem.at[14]),
    ]
    for copy in locs:
        copy.start()
    early()
    locs[0].wait()
    locs[1].wait()
    sw = sw_own[...].astype(F32)
    M[0] = jnp.concatenate(
        [sw[:, 0:256], sw[:, 256:512]] + [tail_own[k] for k in range(3)] + [jnp.zeros((5, CH), F32)], axis=0
    ).astype(BF)
    locs[2].wait()
    own = state_own[...].astype(BF)
    S[...] = jnp.zeros_like(S)
    for way in (0, 1):
        for part in (0, 1):
            S[way * HELD + part] = own[128 * part : 128 * part + 128]
    for i in range(3, 7):
        locs[i].wait()

    def state_row(q):
        sid = request_state[q]
        return owner_map[jnp.where(sid < Z, sid, shared_id[0])]

    def make_plan():
        pack = lax.broadcasted_iota(jnp.int32, (1, 64), 1)
        way, src, part = pack // 32, (pack % 32) // 2, pack % 2
        most = jnp.where(part == 0, REACH[0], REACH[1])
        togo = jnp.zeros((1, 64), jnp.int32)
        for q in range(Z):
            row = state_row(q)
            d = (q - row + Z) % Z
            ahead = jnp.where((d <= most) & (way == 0), d, 0)
            behind = jnp.where((d > most) & (way == 1), Z - d, 0)
            togo = jnp.maximum(togo, jnp.where(src == row, ahead + behind, 0))
        togo = togo.astype(F32)
        at = src
        name = (src * 2 + part + 1).astype(F32)
        code = (part + 1).astype(F32)
        order = pack.astype(F32)
        link_row = lax.broadcasted_iota(jnp.int32, (32, 64), 0)
        sent, came = [], []
        for t in range(STEPS):
            key = jnp.where(togo > 0.0, togo * 64.0 + order, 0.0)
            here = link_row == at + way * Z
            best = jnp.max(jnp.where(here, key, 0.0), axis=1, keepdims=True)
            wins = here & (key == best) & (key > 0.0)
            win = jnp.max(jnp.where(wins, 1.0, 0.0), axis=0, keepdims=True)
            then = jnp.where(way == 0, (at + 1) % Z, (at + Z - 1) % Z)
            sent.append(jnp.where(at == z, win * code, 0.0))
            came.append(jnp.where(then == z, win * name, 0.0))
            togo = togo - win
            code = jnp.where(win > 0.0, t + 3.0, code)
            at = jnp.where(win > 0.0, then, at)
        rest = [jnp.zeros((Z - STEPS, 64), F32)]
        sent, came = jnp.concatenate(sent + rest, axis=0), jnp.concatenate(came + rest, axis=0)
        half = lax.broadcasted_iota(jnp.int32, (Z, 64), 1) // 32
        lane = lax.broadcasted_iota(jnp.int32, (Z, 128), 1)
        table = jnp.zeros((Z, 128), F32)
        for k, (what, w) in enumerate(((sent, 0), (sent, 1), (came, 0), (came, 1))):
            column = jnp.max(jnp.where(half == w, what, 0.0), axis=1, keepdims=True)
            table = jnp.where(lane == k, column, table)
        plan_v[...] = table.astype(jnp.int32)
        copy = pltpu.make_async_copy(plan_v, plan, plan_sem)
        copy.start()
        copy.wait()

    def convey(t):
        for way in (0, 1):
            if t > 0:
                got(landed.at[way, t - 1], vs_sem.at[way, t - 1], vr_sem.at[way, t - 1], zdev[way])
                S[way * HELD + t + 1] = landed[way, t - 1]
            if t < STEPS:
                k = jnp.clip(plan[t, way] - 1, 0, HELD - 1)
                stage[way, t] = S[way * HELD + k]
                go(stage.at[way, t], vs_sem.at[way, t], vr_sem.at[way, t], zdev[way], landed.at[way, t])

    def prior_half(row, part):
        at = part
        for way in (0, 1):
            for t in range(STEPS):
                at = jnp.where(plan[t, 2 + way] == row * 2 + part + 1, way * HELD + t + 2, at)
        return S[at]

    def m_step(s):
        for way in (0, 1):
            if s < 8 or 0 in last_subs(way, ms_sem):
                ring(M, pl.ds(0, 16), 0, ms_sem, mr_sem, way, s)

    def ring4(stage, blk, halves, nb, s_sem, r_sem):
        if stage == 0:
            for way in (0, 1):
                go(blk(0), s_sem.at[way], r_sem.at[way], nb[way])
        elif stage == 1:
            for way, step in ((0, -1), (1, 1)):
                got(blk(step), s_sem.at[way], r_sem.at[way], nb[way])
                go(halves(blk(step), way), s_sem.at[2 + way], r_sem.at[2 + way], nb[way])
        else:
            for way in (0, 1):
                got(halves(blk(2), way), s_sem.at[2 + way], r_sem.at[2 + way], nb[way])

    def a_one(stage, i):
        p, q = pos[i]
        ring4(
            stage,
            lambda k: A.at[i, c, p, (q + 4 + k) % 4],
            lambda ref, way: ref.at[pl.ds(128 * way, 128)],
            q_nb[i], as_sem.at[i, 0], ar_sem.at[i, 0],
        )

    def a_two(stage, i):
        p, _ = pos[i]

        def part(k, piece):
            return A.at[i, c, (p + 4 + k) % 4, pl.ds(2 * piece, 2)]

        def sems(n, way):
            return as_sem.at[i, 1 + n, way], ar_sem.at[i, 1 + n, way]

        for way, step in ((0, -1), (1, 1)):
            d = p_nb[i][way]
            if stage == 0:
                go(part(0, way), *sems(0, way), d)
                go(part(0, 1 - way), *sems(1, way), d)
            elif stage == 1:
                got(part(step, way), *sems(0, way), d)
                go(part(step, way), *sems(2, way), d)
            elif stage == 2:
                got(part(step, 1 - way), *sems(1, way), d)
            else:
                got(part(2, way), *sems(2, way), d)

    def a_share(i, k):
        p, _ = pos[i]
        go(A.at[i, c, (p + k) % 4], cs_sem.at[i, k], cr_sem.at[i, k], sibling)

    def a_shared(i, k):
        p, _ = pos[i]
        got(A.at[i, 1 - c, (p + k) % 4], cs_sem.at[i, k], cr_sem.at[i, k], sibling)

    def g_ring(stage):
        ring4(
            stage,
            lambda k: G.at[c, (y + 4 + k) % 4],
            lambda ref, way: ref.at[pl.ds(32 * way, 32)],
            y_nb, gs_sem, gr_sem,
        )

    def a_block(i, kz, cc):
        ax, ay = kz // 4, kz % 4
        return A[0, cc, ay, ax] if i == 0 else A[1, cc, ax, ay]

    def project(j):
        kz = (z - j + Z) % Z
        for i in (0, 1):
            rows = pl.ds(256 * i, 256)
            part = jnp.dot(a_block(i, kz, 0), W[j, 0:256], preferred_element_type=F32)
            part += jnp.dot(a_block(i, kz, 1), W[j, 256:512], preferred_element_type=F32)
            acc[rows, :] += part

    def step_part(j):
        kz = (z - j + Z) % Z
        for i in (0, 1):
            for cc in (0, 1):
                sacc[cc, :, pl.ds(256 * i, 256)] += lax.dot_general(
                    M[j], a_block(i, kz, cc), (((1,), (1,)), ((), ())), preferred_element_type=F32
                )

    def vectors():
        for k in range(4):
            inT[pl.ds(64 * k, 64), :] = G[k % 2, k // 2]
            outv[:, pl.ds(64 * k, 64)] = G[k % 2, 2 + k // 2].astype(F32).T.astype(BF)

    def scores(tb):
        t0 = tb * 128
        cols = 256 if tb < 2 else 512
        sc = jnp.dot(outv[pl.ds(t0, 128), :], inT[:, 0:cols], preferred_element_type=F32)
        keep = lax.broadcasted_iota(jnp.int32, (128, cols), 1) <= t0 + lax.broadcasted_iota(jnp.int32, (128, cols), 0)
        score[pl.ds(t0, 128), 0:cols] = jnp.where(keep, sc, 0.0)

    def decays():
        row = lax.broadcasted_iota(jnp.int32, (8, 1), 0)

        def per_head(ref):
            col = jnp.zeros((8, 1), F32)
            for h in range(HEADS):
                col = jnp.where(row == h, ref[h], col)
            return col

        raw = jnp.concatenate([sacc[0, 0:4] + sacc[1, 4:8], jnp.zeros((4, TOK), F32)], axis=0)
        raw = raw + per_head(step_bias)
        step = jnp.maximum(raw, 0.0) + jnp.log1p(jnp.exp(-jnp.abs(raw)))
        decay = -jnp.exp(per_head(decay_log)) * step
        lane = lax.broadcasted_iota(jnp.int32, (8, TOK), 1)
        for k in range(9):
            decay = decay + jnp.where(lane >= 2**k, pltpu.roll(decay, 2**k, axis=1), 0.0)
        last = decay[:, TOK - 1 : TOK]
        weights = jnp.exp(last - decay) * step
        rates[0] = decay
        rates[1] = step
        decay_t = jnp.concatenate([decay, jnp.zeros((120, TOK), F32)], axis=0).T
        grown_t = jnp.exp(decay_t)
        weights_t = jnp.concatenate([weights, jnp.zeros((120, TOK), F32)], axis=0).T
        rate_t[0] = decay_t
        rate_t[1] = grown_t
        rate_t[2] = weights_t

    def make_mix(h):
        for tb in range(4):
            t0 = tb * 128
            cols = 256 if tb < 2 else 512
            differ = rate_t[0, t0 : t0 + 128, h : h + 1] - rates[0, h : h + 1, 0:cols]
            scaled = jnp.exp(jnp.minimum(differ, 0.0)) * rates[1, h : h + 1, 0:cols]
            mix[h, pl.ds(t0, 128), 0:cols] = (score[pl.ds(t0, 128), 0:cols] * scaled).astype(BF)

    def step_parts(first):
        @pl.loop(first, first + 4)
        def _(j):
            step_part(j)

    def projects(first, end):
        @pl.loop(first, end)
        def _(j):
            project(j)
            project(Z - j)

    def g_share():
        go(G.at[c], gs_sem.at[4], gr_sem.at[4], sibling)

    def g_shared():
        got(G.at[1 - c], gs_sem.at[4], gr_sem.at[4], sibling)

    def both(f, *args):
        for i in (0, 1):
            f(*args, i)

    def shared(i):
        for k in range(4):
            a_shared(i, k)

    chan = lax.broadcasted_iota(jnp.int32, (TOK, CH), 1) // 64

    def clear():
        acc[...] = jnp.zeros_like(acc)
        sacc[...] = jnp.zeros_like(sacc)

    def expand(cols):
        wide = jnp.broadcast_to(cols[:, 0:1], (TOK, CH))
        for h in range(1, HEADS):
            wide = jnp.where(chan == h, cols[:, h : h + 1], wide)
        return wide

    def expand_decays():
        base[...] = expand(rate_t[1])
        weigh[...] = expand(rate_t[2])

    def put_tail():
        j = (z - state_row(z) + Z) % Z
        ext[0:8, :] = jnp.concatenate([jnp.zeros((5, CH), F32), M[j].astype(F32)[8:11]], axis=0)

    def resume():
        row = state_row(z)
        prior = jnp.concatenate([prior_half(row, 0), prior_half(row, 1)], axis=0)
        base[...] *= lax.dot_general(outv[...], prior, (((1,), (1,)), ((), ())), preferred_element_type=F32)
        head_row = lax.broadcasted_iota(jnp.int32, (CH, 1), 0) // 64
        kept = jnp.zeros((CH, 1), F32)
        last_e = jnp.exp(rates[0, :, TOK - 1 : TOK])
        for h in range(HEADS):
            kept = jnp.where(head_row == h, last_e[h : h + 1, 0:1], kept)
        carry[...] = kept * prior.astype(F32)

    work = {u: [] for u in range(4 * 9)}

    def add(u, f, *args):
        work[u].append((f, args))

    for t in range(1, STEPS):
        add(2 + 33 * t // STEPS, convey, t)
    for s, u in enumerate((0, 4, 6, 8, 10, 13, 15, 18, 20)):
        if s:
            add(u, m_step, s)
    add(3, clear)
    add(5, both, a_one, 1)
    add(5, g_ring, 1)
    add(7, g_ring, 2)
    add(7, g_share)
    add(8, both, a_one, 2)
    add(8, both, a_two, 0)
    add(8, lambda: both(lambda i: a_share(i, 0)))
    add(11, g_shared)
    add(11, vectors)
    add(13, both, a_two, 1)
    for tb in range(4):
        add(12 + tb, scores, tb)
    add(16, both, a_two, 2)
    add(16, lambda: both(lambda i: (a_share(i, 3), a_share(i, 1))))
    add(19, both, a_two, 3)
    add(19, lambda: both(lambda i: a_share(i, 2)))
    add(21, both, shared)
    for k in range(4):
        add(21 + k, step_parts, 4 * k)
    add(24, decays)
    for h in range(HEADS):
        add(25 + h, make_mix, h)
    add(27, put_tail)
    add(28, expand_decays)
    add(28, project, 0)
    add(29, projects, 1, 3)
    add(30, projects, 3, 5)
    add(31, projects, 5, 7)
    add(32, projects, 7, 8)

    m_step(0)
    both(a_one, 0)
    for i in range(7, 15):
        locs[i].wait()
    make_plan()
    convey(0)
    w_step(0, (2, 3))
    g_ring(0)
    for u in range(3, 36):
        if u > 3:
            w_step(u // 4, (u % 4,))
        for f, args in work[u]:
            f(*args)

    project(8)
    projected = acc[...].astype(BF).astype(F32)
    ext[8 : 8 + TOK, :] = projected
    for k in range(3):
        ftail_ref[k] = ext[TOK + 5 + k : TOK + 6 + k, :]
    conv = conv_b[...] + conv_w[0:1, :] * ext[5 : 5 + TOK, :]
    for k in range(1, 4):
        conv = conv + conv_w[k : k + 1, :] * ext[5 + k : 5 + k + TOK, :]
    conv_f = (conv / (1.0 + jnp.exp(-conv))).astype(BF).astype(F32)
    skip = jnp.zeros((1, CH), F32)
    one = lax.broadcasted_iota(jnp.int32, (1, CH), 1) // 64
    for h in range(HEADS):
        skip = jnp.where(one == h, skip_gain[h], skip)
        xbd[h] = jnp.where(chan == h, conv_f, 0.0).astype(BF)
    for tb in range(2):
        rows = pl.ds(256 * tb, 256)
        cols = 256 * (tb + 1)
        inner = (skip * conv_f)[256 * tb : 256 * tb + 256]
        for h in range(HEADS):
            inner = inner + jnp.dot(mix[h, rows, 0:cols], xbd[h, 0:cols, :], preferred_element_type=F32)
        acc[rows, :] = inner
    weighted = (conv_f * weigh[...]).astype(BF)
    new_t = jnp.dot(inT[...], weighted, preferred_element_type=F32)
    convey(STEPS)
    resume()
    fstate_ref[...] = carry[...] + new_t.T
    for tb in range(2):
        rows = pl.ds(256 * tb, 256)
        out_ref[rows, :] = (acc[rows, :] + base[rows, :]).astype(BF)
    for copy in sends:
        copy.wait_send()


def put(*refs):
    srcs, dsts, sem = refs[0:3], refs[3:6], refs[6]
    copies = [pltpu.make_async_copy(src, dst, sem.at[k]) for k, (src, dst) in enumerate(zip(srcs, dsts))]
    for copy in copies:
        copy.start()
    for copy in copies:
        copy.wait()


def on_device(
    layer_input, proj_weight, step_weight, step_bias, decay_log, conv_weight, conv_bias, skip_gain,
    group_inputs, cached_state, cached_tail, owner_map, request_state, shared_id,
):
    smem = pl.BlockSpec(memory_space=pltpu.SMEM)
    vmem = pl.BlockSpec(memory_space=pltpu.VMEM)
    hbm = pl.BlockSpec(memory_space=pl.ANY)
    dma = pltpu.SemaphoreType.DMA
    shapes = (
        jax.ShapeDtypeStruct((TOK, CH), BF),
        jax.ShapeDtypeStruct((CH, N), F32),
        jax.ShapeDtypeStruct((3, 1, CH), F32),
    )
    args = (
        request_state, owner_map, shared_id, step_bias, decay_log, skip_gain,
        layer_input, proj_weight, step_weight.T, cached_tail.transpose(1, 0, 2), cached_state.reshape(CH, N), group_inputs.T,
        conv_weight, conv_bias.reshape(1, CH),
    )

    results = pl.pallas_call(
        body,
        out_shape=shapes,
        in_specs=[hbm] * 14,
        out_specs=(vmem, vmem, vmem),
        scratch_shapes=[
            pltpu.SMEM((16,), jnp.int32),
            pltpu.SMEM((16,), jnp.int32),
            pltpu.SMEM((1,), jnp.int32),
            pltpu.SMEM((4,), F32),
            pltpu.SMEM((4,), F32),
            pltpu.SMEM((4,), F32),
            pltpu.VMEM((4, 256), F32),
            pltpu.VMEM((1, 256), F32),
            pltpu.VMEM((2, 2, 4, 4, 256, 256), BF),
            pltpu.VMEM((Z, 512, 256), BF),
            pltpu.VMEM((2 * HELD, 128, 256), BF),
            pltpu.VMEM((Z, 16, 256), BF),
            pltpu.VMEM((2, 4, 64, 512), BF),
            pltpu.VMEM((2, STEPS, 128, 256), BF),
            pltpu.VMEM((2, STEPS, 128, 256), BF),
            pltpu.VMEM((Z, 128), jnp.int32),
            pltpu.SMEM((Z, 128), jnp.int32),
            pltpu.VMEM((256, 256), F32),
            pltpu.VMEM((4, 512), BF),
            pltpu.VMEM((3, 1, 256), F32),
            pltpu.VMEM((512, 256), F32),
            pltpu.VMEM((2, 16, 512), F32),
            pltpu.VMEM((8 + TOK, 256), F32),
            pltpu.VMEM((256, 512), BF),
            pltpu.VMEM((512, 256), BF),
            pltpu.VMEM((512, 512), F32),
            pltpu.VMEM((4, 512, 512), BF),
            pltpu.VMEM((4, 512, 256), BF),
            pltpu.VMEM((2, 8, 512), F32),
            pltpu.VMEM((3, 512, 128), F32),
            pltpu.VMEM((512, 256), F32),
            pltpu.VMEM((512, 256), F32),
            pltpu.VMEM((256, 256), F32),
            dma((15,)),
            dma((2, 8, WSUB)),
            dma((2, 8, WSUB)),
            dma((2, 8, 1)),
            dma((2, 8, 1)),
            dma((2, 4, 4)),
            dma((2, 4, 4)),
            dma((2, 4)),
            dma((2, 4)),
            dma((5,)),
            dma((5,)),
            dma((2, STEPS)),
            dma((2, STEPS)),
            dma,
        ],
        compiler_params=pltpu.CompilerParams(
            collective_id=0, has_side_effects=True, vmem_limit_bytes=56 * 1024 * 1024
        ),
    )(*args)

    results = lax.cond(shared_id[0] >= 0, lambda *v: v, lambda *v: tuple(jnp.zeros_like(u) for u in v), *results)
    out, fstate, ftail = pl.pallas_call(
        put, out_shape=shapes, in_specs=[vmem] * 3, out_specs=[hbm] * 3, scratch_shapes=[dma((3,))]
    )(*results)
    return out, fstate.reshape(1, HEADS, 64, N), ftail.transpose(1, 0, 2)


def solution(mesh):
    return jax.shard_map(
        on_device,
        mesh=mesh,
        in_specs=(
            P("rep", "head"), P("rep", "head"), P("rep", "head"), P("head"), P("head"), P(None, "head"),
            P("head"), P("head"), P("rep", "head"), P("rep", "head", None, None), P("rep", None, "head"),
            P(), P(), P(),
        ),
        out_specs=(P("rep", "head"), P("rep", "head", None, None), P("rep", None, "head")),
        check_vma=False,
    )
```

```python
import jax
import jax.numpy as jnp
from jax import lax
from jax.experimental import pallas as pl
from jax.experimental.pallas import tpu as pltpu
from jax.sharding import PartitionSpec as P

MESH = pl.DeviceIdType.MESH
BF = jnp.bfloat16
F32 = jnp.float32
Z = 16
TOK = 512
CH = 256
HEADS = 4
N = 256
WSUB = 4
STEPS = 10
HELD = STEPS + 2
REACH = (10, 5)


def body(
    request_hbm, owner_hbm, shared_hbm, bias_hbm, decay_hbm, gain_hbm,
    x_hbm, w_hbm, sw_hbm, tail_hbm, state_hbm, g_hbm, cw_hbm, cb_hbm,
    out_ref, fstate_ref, ftail_ref,
    request_state, owner_map, shared_id, step_bias, decay_log, skip_gain, conv_w, conv_b,
    A, W, S, M, G, stage, landed, plan_v, plan, state_own, sw_own, tail_own, acc, sacc, ext, inT, outv, score, mix, xbd, rates, rate_t, base, weigh, carry,
    loc_sem, ws_sem, wr_sem, ms_sem, mr_sem, as_sem, ar_sem, cs_sem, cr_sem, gs_sem, gr_sem, vs_sem, vr_sem, plan_sem,
):
    z = lax.axis_index("rep")
    hid = lax.axis_index("head")
    x, y, c = hid // 8, (hid // 2) % 4, hid % 2
    zr, zl = (z + 1) % Z, (z + Z - 1) % Z

    def dev(xx, yy, cc):
        return {"head": xx * 8 + yy * 2 + cc}

    xp, xm, yp, ym = (x + 1) % 4, (x + 3) % 4, (y + 1) % 4, (y + 3) % 4
    sibling = dev(x, y, 1 - c)
    zdev = ({"rep": zr}, {"rep": zl})
    pos = ((y, x), (x, y))
    x_nb, y_nb = (dev(xp, y, c), dev(xm, y, c)), (dev(x, yp, c), dev(x, ym, c))
    q_nb, p_nb = (x_nb, y_nb), (y_nb, x_nb)

    barrier = pltpu.get_barrier_semaphore()
    for d in (*zdev, *x_nb, *y_nb, sibling):
        pl.semaphore_signal(barrier, inc=1, device_id=d, device_id_type=MESH)

    sends = []

    def rcopy(src, dst, s_sem, r_sem, d):
        return pltpu.make_async_remote_copy(
            src_ref=src, dst_ref=dst, send_sem=s_sem, recv_sem=r_sem, device_id=d, device_id_type=MESH
        )

    def go(ref, s_sem, r_sem, d, dst=None):
        copy = rcopy(ref, ref if dst is None else dst, s_sem, r_sem, d)
        copy.start()
        sends.append(copy)

    def got(ref, s_sem, r_sem, d):
        rcopy(ref, ref, s_sem, r_sem, d).wait_recv()

    def slot(way, s):
        return s if way == 0 else (Z - s) % Z

    def ring(buf, rows, sub, s_sem, r_sem, way, s):
        here = buf.at[slot(way, s), rows]
        if s > 0:
            got(here, s_sem.at[way, s - 1, sub], r_sem.at[way, s - 1, sub], zdev[way])
        if s < 8 and not (s == 7 and sub not in last_subs(way, s_sem)):
            go(here, s_sem.at[way, s, sub], r_sem.at[way, s, sub], zdev[way], buf.at[slot(way, s + 1), rows])

    def last_subs(way, s_sem):
        if s_sem is ws_sem:
            return (0, 1) if way == 0 else (2, 3)
        return (0,) if way == 0 else ()

    def w_step(s, subs=range(WSUB)):
        for sub in subs:
            for way in (0, 1):
                if s < 8 or sub in last_subs(way, ws_sem):
                    ring(W, pl.ds(sub * (512 // WSUB), 512 // WSUB), sub, ws_sem, wr_sem, way, s)

    def early():
        pl.semaphore_wait(barrier, 7)
        for sub in (0, 1):
            rows = pl.ds(128 * sub, 128)
            for way in (0, 1):
                go(w_hbm.at[rows], ws_sem.at[way, 0, sub], wr_sem.at[way, 0, sub], zdev[way], W.at[slot(way, 1), rows])

    locs = [
        pltpu.make_async_copy(sw_hbm, sw_own, loc_sem.at[0]),
        pltpu.make_async_copy(tail_hbm, tail_own, loc_sem.at[1]),
        pltpu.make_async_copy(state_hbm, state_own, loc_sem.at[2]),
        pltpu.make_async_copy(w_hbm, W.at[0], loc_sem.at[3]),
        pltpu.make_async_copy(x_hbm.at[0:256], A.at[0, c, y, x], loc_sem.at[4]),
        pltpu.make_async_copy(x_hbm.at[256:512], A.at[1, c, x, y], loc_sem.at[5]),
        pltpu.make_async_copy(g_hbm, G.at[c, y], loc_sem.at[6]),
        pltpu.make_async_copy(request_hbm, request_state, loc_sem.at[7]),
        pltpu.make_async_copy(owner_hbm, owner_map, loc_sem.at[8]),
        pltpu.make_async_copy(shared_hbm, shared_id, loc_sem.at[9]),
        pltpu.make_async_copy(bias_hbm, step_bias, loc_sem.at[10]),
        pltpu.make_async_copy(decay_hbm, decay_log, loc_sem.at[11]),
        pltpu.make_async_copy(gain_hbm, skip_gain, loc_sem.at[12]),
        pltpu.make_async_copy(cw_hbm, conv_w, loc_sem.at[13]),
        pltpu.make_async_copy(cb_hbm, conv_b, loc_sem.at[14]),
    ]
    for copy in locs:
        copy.start()
    early()
    locs[0].wait()
    locs[1].wait()
    sw = sw_own[...].astype(F32)
    M[0] = jnp.concatenate(
        [sw[:, 0:256], sw[:, 256:512]] + [tail_own[k] for k in range(3)] + [jnp.zeros((5, CH), F32)], axis=0
    ).astype(BF)
    locs[2].wait()
    own = state_own[...].astype(BF)
    S[...] = jnp.zeros_like(S)
    for way in (0, 1):
        for part in (0, 1):
            S[way * HELD + part] = own[128 * part : 128 * part + 128]
    for i in range(3, 7):
        locs[i].wait()

    def state_row(q):
        sid = request_state[q]
        return owner_map[jnp.where(sid < Z, sid, shared_id[0])]

    def make_plan():
        pack = lax.broadcasted_iota(jnp.int32, (1, 64), 1)
        way, src, part = pack // 32, (pack % 32) // 2, pack % 2
        most = jnp.where(part == 0, REACH[0], REACH[1])
        togo = jnp.zeros((1, 64), jnp.int32)
        for q in range(Z):
            row = state_row(q)
            d = (q - row + Z) % Z
            ahead = jnp.where((d <= most) & (way == 0), d, 0)
            behind = jnp.where((d > most) & (way == 1), Z - d, 0)
            togo = jnp.maximum(togo, jnp.where(src == row, ahead + behind, 0))
        togo = togo.astype(F32)
        at = src
        name = (src * 2 + part + 1).astype(F32)
        code = (part + 1).astype(F32)
        order = pack.astype(F32)
        link_row = lax.broadcasted_iota(jnp.int32, (32, 64), 0)
        sent, came = [], []
        for t in range(STEPS):
            key = jnp.where(togo > 0.0, togo * 64.0 + order, 0.0)
            here = link_row == at + way * Z
            best = jnp.max(jnp.where(here, key, 0.0), axis=1, keepdims=True)
            wins = here & (key == best) & (key > 0.0)
            win = jnp.max(jnp.where(wins, 1.0, 0.0), axis=0, keepdims=True)
            then = jnp.where(way == 0, (at + 1) % Z, (at + Z - 1) % Z)
            sent.append(jnp.where(at == z, win * code, 0.0))
            came.append(jnp.where(then == z, win * name, 0.0))
            togo = togo - win
            code = jnp.where(win > 0.0, t + 3.0, code)
            at = jnp.where(win > 0.0, then, at)
        rest = [jnp.zeros((Z - STEPS, 64), F32)]
        sent, came = jnp.concatenate(sent + rest, axis=0), jnp.concatenate(came + rest, axis=0)
        half = lax.broadcasted_iota(jnp.int32, (Z, 64), 1) // 32
        lane = lax.broadcasted_iota(jnp.int32, (Z, 128), 1)
        table = jnp.zeros((Z, 128), F32)
        for k, (what, w) in enumerate(((sent, 0), (sent, 1), (came, 0), (came, 1))):
            column = jnp.max(jnp.where(half == w, what, 0.0), axis=1, keepdims=True)
            table = jnp.where(lane == k, column, table)
        plan_v[...] = table.astype(jnp.int32)
        copy = pltpu.make_async_copy(plan_v, plan, plan_sem)
        copy.start()
        copy.wait()

    def convey(t):
        for way in (0, 1):
            if t > 0:
                got(landed.at[way, t - 1], vs_sem.at[way, t - 1], vr_sem.at[way, t - 1], zdev[way])
                S[way * HELD + t + 1] = landed[way, t - 1]
            if t < STEPS:
                k = jnp.clip(plan[t, way] - 1, 0, HELD - 1)
                stage[way, t] = S[way * HELD + k]
                go(stage.at[way, t], vs_sem.at[way, t], vr_sem.at[way, t], zdev[way], landed.at[way, t])

    def prior_half(row, part):
        at = part
        for way in (0, 1):
            for t in range(STEPS):
                at = jnp.where(plan[t, 2 + way] == row * 2 + part + 1, way * HELD + t + 2, at)
        return S[at]

    def m_step(s):
        for way in (0, 1):
            if s < 8 or 0 in last_subs(way, ms_sem):
                ring(M, pl.ds(0, 16), 0, ms_sem, mr_sem, way, s)

    def ring4(stage, blk, halves, nb, s_sem, r_sem):
        if stage == 0:
            for way in (0, 1):
                go(blk(0), s_sem.at[way], r_sem.at[way], nb[way])
        elif stage == 1:
            for way, step in ((0, -1), (1, 1)):
                got(blk(step), s_sem.at[way], r_sem.at[way], nb[way])
                go(halves(blk(step), way), s_sem.at[2 + way], r_sem.at[2 + way], nb[way])
        else:
            for way in (0, 1):
                got(halves(blk(2), way), s_sem.at[2 + way], r_sem.at[2 + way], nb[way])

    def a_one(stage, i):
        p, q = pos[i]
        ring4(
            stage,
            lambda k: A.at[i, c, p, (q + 4 + k) % 4],
            lambda ref, way: ref.at[pl.ds(128 * way, 128)],
            q_nb[i], as_sem.at[i, 0], ar_sem.at[i, 0],
        )

    def a_two(stage, i):
        p, _ = pos[i]

        def part(k, piece):
            return A.at[i, c, (p + 4 + k) % 4, pl.ds(2 * piece, 2)]

        def sems(n, way):
            return as_sem.at[i, 1 + n, way], ar_sem.at[i, 1 + n, way]

        for way, step in ((0, -1), (1, 1)):
            d = p_nb[i][way]
            if stage == 0:
                go(part(0, way), *sems(0, way), d)
                go(part(0, 1 - way), *sems(1, way), d)
            elif stage == 1:
                got(part(step, way), *sems(0, way), d)
                go(part(step, way), *sems(2, way), d)
            elif stage == 2:
                got(part(step, 1 - way), *sems(1, way), d)
            else:
                got(part(2, way), *sems(2, way), d)

    def a_share(i, k):
        p, _ = pos[i]
        go(A.at[i, c, (p + k) % 4], cs_sem.at[i, k], cr_sem.at[i, k], sibling)

    def a_shared(i, k):
        p, _ = pos[i]
        got(A.at[i, 1 - c, (p + k) % 4], cs_sem.at[i, k], cr_sem.at[i, k], sibling)

    def g_ring(stage):
        ring4(
            stage,
            lambda k: G.at[c, (y + 4 + k) % 4],
            lambda ref, way: ref.at[pl.ds(32 * way, 32)],
            y_nb, gs_sem, gr_sem,
        )

    def a_block(i, kz, cc):
        ax, ay = kz // 4, kz % 4
        return A[0, cc, ay, ax] if i == 0 else A[1, cc, ax, ay]

    def project(j):
        kz = (z - j + Z) % Z
        for i in (0, 1):
            rows = pl.ds(256 * i, 256)
            part = jnp.dot(a_block(i, kz, 0), W[j, 0:256], preferred_element_type=F32)
            part += jnp.dot(a_block(i, kz, 1), W[j, 256:512], preferred_element_type=F32)
            acc[rows, :] += part

    def step_part(j):
        kz = (z - j + Z) % Z
        for i in (0, 1):
            for cc in (0, 1):
                sacc[cc, :, pl.ds(256 * i, 256)] += lax.dot_general(
                    M[j], a_block(i, kz, cc), (((1,), (1,)), ((), ())), preferred_element_type=F32
                )

    def vectors():
        for k in range(4):
            inT[pl.ds(64 * k, 64), :] = G[k % 2, k // 2]
            outv[:, pl.ds(64 * k, 64)] = G[k % 2, 2 + k // 2].astype(F32).T.astype(BF)

    def scores(tb):
        t0 = tb * 128
        cols = 256 if tb < 2 else 512
        sc = jnp.dot(outv[pl.ds(t0, 128), :], inT[:, 0:cols], preferred_element_type=F32)
        keep = lax.broadcasted_iota(jnp.int32, (128, cols), 1) <= t0 + lax.broadcasted_iota(jnp.int32, (128, cols), 0)
        score[pl.ds(t0, 128), 0:cols] = jnp.where(keep, sc, 0.0)

    def decays():
        row = lax.broadcasted_iota(jnp.int32, (8, 1), 0)

        def per_head(ref):
            col = jnp.zeros((8, 1), F32)
            for h in range(HEADS):
                col = jnp.where(row == h, ref[h], col)
            return col

        raw = jnp.concatenate([sacc[0, 0:4] + sacc[1, 4:8], jnp.zeros((4, TOK), F32)], axis=0)
        raw = raw + per_head(step_bias)
        step = jnp.maximum(raw, 0.0) + jnp.log1p(jnp.exp(-jnp.abs(raw)))
        decay = -jnp.exp(per_head(decay_log)) * step
        lane = lax.broadcasted_iota(jnp.int32, (8, TOK), 1)
        for k in range(9):
            decay = decay + jnp.where(lane >= 2**k, pltpu.roll(decay, 2**k, axis=1), 0.0)
        last = decay[:, TOK - 1 : TOK]
        weights = jnp.exp(last - decay) * step
        rates[0] = decay
        rates[1] = step
        decay_t = jnp.concatenate([decay, jnp.zeros((120, TOK), F32)], axis=0).T
        grown_t = jnp.exp(decay_t)
        weights_t = jnp.concatenate([weights, jnp.zeros((120, TOK), F32)], axis=0).T
        rate_t[0] = decay_t
        rate_t[1] = grown_t
        rate_t[2] = weights_t

    def make_mix(h):
        for tb in range(4):
            t0 = tb * 128
            cols = 256 if tb < 2 else 512
            differ = rate_t[0, t0 : t0 + 128, h : h + 1] - rates[0, h : h + 1, 0:cols]
            scaled = jnp.exp(jnp.minimum(differ, 0.0)) * rates[1, h : h + 1, 0:cols]
            mix[h, pl.ds(t0, 128), 0:cols] = (score[pl.ds(t0, 128), 0:cols] * scaled).astype(BF)

    def step_parts(first):
        @pl.loop(first, first + 4)
        def _(j):
            step_part(j)

    def projects(first, end):
        @pl.loop(first, end)
        def _(j):
            project(j)
            project(Z - j)

    def g_share():
        go(G.at[c], gs_sem.at[4], gr_sem.at[4], sibling)

    def g_shared():
        got(G.at[1 - c], gs_sem.at[4], gr_sem.at[4], sibling)

    def both(f, *args):
        for i in (0, 1):
            f(*args, i)

    def shared(i):
        for k in range(4):
            a_shared(i, k)

    chan = lax.broadcasted_iota(jnp.int32, (TOK, CH), 1) // 64

    def clear():
        acc[...] = jnp.zeros_like(acc)
        sacc[...] = jnp.zeros_like(sacc)

    def expand(cols):
        wide = jnp.broadcast_to(cols[:, 0:1], (TOK, CH))
        for h in range(1, HEADS):
            wide = jnp.where(chan == h, cols[:, h : h + 1], wide)
        return wide

    def expand_decays():
        base[...] = expand(rate_t[1])
        weigh[...] = expand(rate_t[2])

    def put_tail():
        j = (z - state_row(z) + Z) % Z
        ext[0:8, :] = jnp.concatenate([jnp.zeros((5, CH), F32), M[j].astype(F32)[8:11]], axis=0)

    def resume():
        row = state_row(z)
        prior = jnp.concatenate([prior_half(row, 0), prior_half(row, 1)], axis=0)
        base[...] *= lax.dot_general(outv[...], prior, (((1,), (1,)), ((), ())), preferred_element_type=F32)
        head_row = lax.broadcasted_iota(jnp.int32, (CH, 1), 0) // 64
        kept = jnp.zeros((CH, 1), F32)
        last_e = jnp.exp(rates[0, :, TOK - 1 : TOK])
        for h in range(HEADS):
            kept = jnp.where(head_row == h, last_e[h : h + 1, 0:1], kept)
        carry[...] = kept * prior.astype(F32)

    work = {u: [] for u in range(4 * 9)}

    def add(u, f, *args):
        work[u].append((f, args))

    for t in range(1, STEPS):
        add(2 + 31 * t // STEPS, convey, t)
    for s, u in enumerate((0, 4, 6, 8, 10, 13, 15, 18, 20)):
        if s:
            add(u, m_step, s)
    add(3, clear)
    add(5, both, a_one, 1)
    add(5, g_ring, 1)
    add(7, g_ring, 2)
    add(7, g_share)
    add(8, both, a_one, 2)
    add(8, both, a_two, 0)
    add(8, lambda: both(lambda i: a_share(i, 0)))
    add(11, g_shared)
    add(11, vectors)
    add(13, both, a_two, 1)
    for tb in range(4):
        add(12 + tb, scores, tb)
    add(16, both, a_two, 2)
    add(16, lambda: both(lambda i: (a_share(i, 3), a_share(i, 1))))
    add(19, both, a_two, 3)
    add(19, lambda: both(lambda i: a_share(i, 2)))
    add(21, both, shared)
    for k in range(4):
        add(21 + k, step_parts, 4 * k)
    add(24, decays)
    for h in range(HEADS):
        add(25 + h, make_mix, h)
    add(27, put_tail)
    add(28, expand_decays)
    add(28, project, 0)
    add(29, projects, 1, 3)
    add(30, projects, 3, 5)
    add(31, projects, 5, 7)
    add(32, projects, 7, 8)

    m_step(0)
    both(a_one, 0)
    for i in range(7, 15):
        locs[i].wait()
    make_plan()
    convey(0)
    w_step(0, (2, 3))
    g_ring(0)
    for u in range(3, 36):
        if u > 3:
            w_step(u // 4, ((0, 2, 1, 3)[u % 4],))
        for f, args in work[u]:
            f(*args)

    project(8)
    projected = acc[...].astype(BF).astype(F32)
    ext[8 : 8 + TOK, :] = projected
    for k in range(3):
        ftail_ref[k] = ext[TOK + 5 + k : TOK + 6 + k, :]
    conv = conv_b[...] + conv_w[0:1, :] * ext[5 : 5 + TOK, :]
    for k in range(1, 4):
        conv = conv + conv_w[k : k + 1, :] * ext[5 + k : 5 + k + TOK, :]
    conv_f = (conv / (1.0 + jnp.exp(-conv))).astype(BF).astype(F32)
    skip = jnp.zeros((1, CH), F32)
    one = lax.broadcasted_iota(jnp.int32, (1, CH), 1) // 64
    for h in range(HEADS):
        skip = jnp.where(one == h, skip_gain[h], skip)
        xbd[h] = jnp.where(chan == h, conv_f, 0.0).astype(BF)
    for tb in range(2):
        rows = pl.ds(256 * tb, 256)
        cols = 256 * (tb + 1)
        inner = (skip * conv_f)[256 * tb : 256 * tb + 256]
        for h in range(HEADS):
            inner = inner + jnp.dot(mix[h, rows, 0:cols], xbd[h, 0:cols, :], preferred_element_type=F32)
        acc[rows, :] = inner
    weighted = (conv_f * weigh[...]).astype(BF)
    new_t = jnp.dot(inT[...], weighted, preferred_element_type=F32)
    convey(STEPS)
    resume()
    fstate_ref[...] = carry[...] + new_t.T
    for tb in range(2):
        rows = pl.ds(256 * tb, 256)
        out_ref[rows, :] = (acc[rows, :] + base[rows, :]).astype(BF)
    for copy in sends:
        copy.wait_send()


def put(*refs):
    srcs, dsts, sem = refs[0:3], refs[3:6], refs[6]
    copies = [pltpu.make_async_copy(src, dst, sem.at[k]) for k, (src, dst) in enumerate(zip(srcs, dsts))]
    for copy in copies:
        copy.start()
    for copy in copies:
        copy.wait()


def on_device(
    layer_input, proj_weight, step_weight, step_bias, decay_log, conv_weight, conv_bias, skip_gain,
    group_inputs, cached_state, cached_tail, owner_map, request_state, shared_id,
):
    smem = pl.BlockSpec(memory_space=pltpu.SMEM)
    vmem = pl.BlockSpec(memory_space=pltpu.VMEM)
    hbm = pl.BlockSpec(memory_space=pl.ANY)
    dma = pltpu.SemaphoreType.DMA
    shapes = (
        jax.ShapeDtypeStruct((TOK, CH), BF),
        jax.ShapeDtypeStruct((CH, N), F32),
        jax.ShapeDtypeStruct((3, 1, CH), F32),
    )
    args = (
        request_state, owner_map, shared_id, step_bias, decay_log, skip_gain,
        layer_input, proj_weight, step_weight.T, cached_tail.transpose(1, 0, 2), cached_state.reshape(CH, N), group_inputs.T,
        conv_weight, conv_bias.reshape(1, CH),
    )

    results = pl.pallas_call(
        body,
        out_shape=shapes,
        in_specs=[hbm] * 14,
        out_specs=(vmem, vmem, vmem),
        scratch_shapes=[
            pltpu.SMEM((16,), jnp.int32),
            pltpu.SMEM((16,), jnp.int32),
            pltpu.SMEM((1,), jnp.int32),
            pltpu.SMEM((4,), F32),
            pltpu.SMEM((4,), F32),
            pltpu.SMEM((4,), F32),
            pltpu.VMEM((4, 256), F32),
            pltpu.VMEM((1, 256), F32),
            pltpu.VMEM((2, 2, 4, 4, 256, 256), BF),
            pltpu.VMEM((Z, 512, 256), BF),
            pltpu.VMEM((2 * HELD, 128, 256), BF),
            pltpu.VMEM((Z, 16, 256), BF),
            pltpu.VMEM((2, 4, 64, 512), BF),
            pltpu.VMEM((2, STEPS, 128, 256), BF),
            pltpu.VMEM((2, STEPS, 128, 256), BF),
            pltpu.VMEM((Z, 128), jnp.int32),
            pltpu.SMEM((Z, 128), jnp.int32),
            pltpu.VMEM((256, 256), F32),
            pltpu.VMEM((4, 512), BF),
            pltpu.VMEM((3, 1, 256), F32),
            pltpu.VMEM((512, 256), F32),
            pltpu.VMEM((2, 16, 512), F32),
            pltpu.VMEM((8 + TOK, 256), F32),
            pltpu.VMEM((256, 512), BF),
            pltpu.VMEM((512, 256), BF),
            pltpu.VMEM((512, 512), F32),
            pltpu.VMEM((4, 512, 512), BF),
            pltpu.VMEM((4, 512, 256), BF),
            pltpu.VMEM((2, 8, 512), F32),
            pltpu.VMEM((3, 512, 128), F32),
            pltpu.VMEM((512, 256), F32),
            pltpu.VMEM((512, 256), F32),
            pltpu.VMEM((256, 256), F32),
            dma((15,)),
            dma((2, 8, WSUB)),
            dma((2, 8, WSUB)),
            dma((2, 8, 1)),
            dma((2, 8, 1)),
            dma((2, 4, 4)),
            dma((2, 4, 4)),
            dma((2, 4)),
            dma((2, 4)),
            dma((5,)),
            dma((5,)),
            dma((2, STEPS)),
            dma((2, STEPS)),
            dma,
        ],
        compiler_params=pltpu.CompilerParams(
            collective_id=0, has_side_effects=True, vmem_limit_bytes=56 * 1024 * 1024
        ),
    )(*args)

    results = lax.cond(shared_id[0] >= 0, lambda *v: v, lambda *v: tuple(jnp.zeros_like(u) for u in v), *results)
    out, fstate, ftail = pl.pallas_call(
        put, out_shape=shapes, in_specs=[vmem] * 3, out_specs=[hbm] * 3, scratch_shapes=[dma((3,))]
    )(*results)
    return out, fstate.reshape(1, HEADS, 64, N), ftail.transpose(1, 0, 2)


def solution(mesh):
    return jax.shard_map(
        on_device,
        mesh=mesh,
        in_specs=(
            P("rep", "head"), P("rep", "head"), P("rep", "head"), P("head"), P("head"), P(None, "head"),
            P("head"), P("head"), P("rep", "head"), P("rep", "head", None, None), P("rep", None, "head"),
            P(), P(), P(),
        ),
        out_specs=(P("rep", "head"), P("rep", "head", None, None), P("rep", None, "head")),
        check_vma=False,
    )
```
